256 devices in a mesh: grp: 16 (over x_hi, z), band: 16 (over y, x_lo, core).
Axes of the slice: x: 4 (x_hi: 2, x_lo: 2; x = x_hi * 2 + x_lo), y: 4, z: 8, core: 2. Of those that a mesh axis runs over, the one named last changes fastest.
Arguments:
- state: float32 [80, 384, 1280], P('grp', 'band'), may hold values from -6 to 6
- pair_of_slot: int32 [256], replicated, may hold values from 0 to 255, each once
- legendre: float32 [256, 513, 384], P(('grp', 'band')), may hold values from -0.3125 to 0.3125
- diffusion: float32 [80], replicated, may hold values from 0.5 to 8
- w_in: bfloat16 [80, 1024], replicated, may hold values from -0.625 to 0.625
- w_out: bfloat16 [1024, 80], replicated, may hold values from -0.1875 to 0.1875
Outputs:
- new_state: float32 [80, 384, 1280], P('grp', 'band')
The draws below stay inside these ranges and needn't reach their ends.
Inputs may be any that keep to these rules, and one draw needn't show every extreme that they name: `pair_of_slot`: each pair index appears in exactly one slot.
All inputs are finite; a program needn't handle non-finite values.
Results may differ from the reference program's by a relative error of at most 0.004.
Values may be sent and summed in bfloat16 or wider, within the bound.
A program may use at most 64 MiB of HBM per device.

```python
import math
import jax
import jax.numpy as jnp
from jax import lax

C = 80
NLAT = 384
NLON = 1280
M = 512
HIDDEN_SIZE = 1024
PAIRS = 256


def steps_of(stream_key, dims, cuts, least, largest):
    loudness = 1.0
    for axis_at, blocks in cuts:
        draws = jax.random.uniform(jax.random.fold_in(jax.random.fold_in(stream_key, 6), axis_at), (blocks,), jnp.float32, least / len(cuts), largest / len(cuts))
        loudness = loudness * jnp.repeat(jnp.exp(draws), dims[axis_at] // blocks).reshape((-1,) + (1,) * (len(dims) - 1 - axis_at))
    return loudness


def gaussian(rng, extent, deviation, most, pieces=(), kind=jnp.bfloat16):
    result = jax.random.normal(rng, extent, jnp.float32) * deviation
    if len(pieces) > 0:
        result = steps_of(rng, extent, pieces, -0.22, 0.18) * result
    return jnp.clip(result, min=-most, max=most).astype(kind)


def setup_inputs(seed: int = 0) -> dict:
    key_of = jax.random.split(jax.random.key(seed), 7)
    return {
        "state": gaussian(key_of[0], (C, NLAT, NLON), 1.0, 6.0, ((0, 16), (1, 16)), jnp.float32),
        "pair_of_slot": jax.random.permutation(key_of[1], PAIRS).astype(jnp.int32),
        "legendre": gaussian(key_of[2], (PAIRS, M + 1, NLAT), NLAT ** -0.5, 0.3125, ((0, 256),), jnp.float32),
        "diffusion": jnp.clip(jnp.exp(jax.random.uniform(key_of[3], (C,), jnp.float32, math.log(0.5), math.log(8.0))), 0.5, 8.0),
        "w_in": gaussian(key_of[4], (C, HIDDEN_SIZE), C ** -0.5, 0.625),
        "w_out": gaussian(key_of[5], (HIDDEN_SIZE, C), HIDDEN_SIZE ** -0.5, 0.1875),
    }


def fourier_basis(pair_index, points):
    upper_wave = M - 1 - pair_index
    wavenums = jnp.stack([pair_index, pair_index, upper_wave, upper_wave], axis=1).astype(jnp.int32)
    longitude = jnp.arange(points, dtype=jnp.int32)
    phases = (wavenums[:, :, None] * longitude[None, None, :]) % points
    angles = phases.astype(jnp.float32) * jnp.float32(2.0 * math.pi / points)
    cosine = jnp.cos(angles)
    sine_part = jnp.sin(angles)
    parity = (jnp.arange(4, dtype=jnp.int32) % 2 == 0)[None, :, None]
    forward = jnp.where(parity, cosine, -sine_part) / jnp.float32(points)
    weights = jnp.where(wavenums == 0, jnp.float32(1.0), jnp.float32(2.0))[:, :, None]
    inverse = jnp.where(parity, cosine, -sine_part) * weights
    return forward, inverse


def spectral_step(fields, legendre, pair_index, diffusion):
    projected = jnp.einsum("kjcl,krl->kjcr", fields, legendre, precision=lax.Precision.HIGHEST)
    row_index = jnp.arange(legendre.shape[1], dtype=jnp.int32)
    first_part = row_index[None, :] < (M - pair_index)[:, None]
    degree = jnp.where(first_part, pair_index[:, None] + row_index[None, :], row_index[None, :] - 1).astype(jnp.float32)
    scaled = degree * (degree + 1.0) / jnp.float32(M * (M + 1))
    damping = jnp.exp(-diffusion[None, :, None] * scaled[:, None, :])
    keep_first = first_part[:, None, None, :]
    filtered = jnp.where(keep_first, projected[:, 0:2], projected[:, 2:4]) * damping[:, None]
    nothing = jnp.zeros_like(filtered)
    coeffs = jnp.concatenate([jnp.where(keep_first, filtered, nothing), jnp.where(keep_first, nothing, filtered)], axis=1)
    return jnp.einsum("kjcr,krl->kjcl", coeffs, legendre, precision=lax.Precision.HIGHEST)


def reference(state, pair_of_slot, legendre, diffusion, w_in, w_out):
    forward, inverse = fourier_basis(pair_of_slot, NLON)
    coeffs = jnp.einsum("pjn,cln->pjcl", forward, state, precision=lax.Precision.HIGHEST)

    def per_pair(inputs):
        block, table_rows, pair_index = inputs
        return spectral_step(block[None], table_rows[None], pair_index[None], diffusion)[0]

    grid_coeffs = lax.map(per_pair, (coeffs, legendre, pair_of_slot))
    dynamics = jnp.einsum("pjcl,pjn->cln", grid_coeffs, inverse, precision=lax.Precision.HIGHEST)

    def column_physics(block):
        inputs_low = block.astype(jnp.bfloat16)
        hidden = lax.dot_general(w_in, inputs_low, (((0,), (0,)), ((), ())), preferred_element_type=jnp.float32)
        hidden = jax.nn.silu(hidden).astype(jnp.bfloat16)
        return lax.dot_general(w_out, hidden, (((0,), (0,)), ((), ())), preferred_element_type=jnp.float32)

    tendency = lax.map(column_physics, jnp.moveaxis(state, 1, 0))
    return dynamics + jnp.moveaxis(tendency, 0, 1)
```

```python
import math

import jax
import jax.numpy as jnp
import numpy as np
from jax import lax
from jax.experimental import pallas as pl
from jax.experimental.pallas import tpu as pltpu
from jax.sharding import PartitionSpec as P

NLON = 1280
HALF = NLON // 2
M = 512
C5 = 5
LAT = 24
N = 16
ROWS = 528
TILES = 15
F32 = jnp.float32
BF16 = jnp.bfloat16


def transform_table():
    q = np.arange(128)
    lon = np.arange(HALF)
    blocks = []
    for parity in (0, 1):
        for j in range(4):
            p = 2 * q + (parity if j < 2 else 1 - parity)
            m = p if j < 2 else M - 1 - p
            phase = 2.0 * np.pi * ((m[:, None] * lon[None, :]) % NLON) / NLON
            blocks.append(np.cos(phase) if j % 2 == 0 else -np.sin(phase))
    return np.concatenate(blocks, 0).astype(jnp.bfloat16)


def kernel(
    state_h, pair_s, pair_v, leg_h, diff_s, win_h, wout_h, tab_h,
    out_ref,
    st, tab, leg, win, wout,
    s_send, s_recv, t_send, t_recv,
    f1_send, f1_recv, f2_send, f2_recv,
    b1_send, b1_recv, b2_send, b2_recv,
    mid, phys, xb, zf, fac, legb, legt, wint, woutt, ohf, oh, ohbg,
    load_sem, s_ss, s_rs, t_ss, t_rs, f1_ss, f1_rs, f2_ss, f2_rs, b1_ss, b1_rs, b2_ss, b2_rs,
):
    g = lax.axis_index("grp")
    b = lax.axis_index("band")

    loads = [
        pltpu.make_async_copy(src, dst, load_sem.at[i])
        for i, (src, dst) in enumerate(
            [(state_h, st), (tab_h, tab), (leg_h.at[0], leg), (win_h, win), (wout_h, wout)]
        )
    ]
    for load in loads:
        load.start()

    barrier = pltpu.get_barrier_semaphore()

    def greet(k, carry):
        pl.semaphore_signal(barrier, inc=1, device_id={"grp": lax.rem(g + k, N)}, device_id_type=pl.DeviceIdType.MESH)
        pl.semaphore_signal(barrier, inc=1, device_id={"band": lax.rem(b + k, N)}, device_id_type=pl.DeviceIdType.MESH)
        return carry

    lax.fori_loop(1, N, greet, 0)

    def exchange(axis, me, src, dst, ss, rs):
        def copy(k):
            other = lax.rem(me + k, N)
            return pltpu.make_async_remote_copy(
                src_ref=src.at[other], dst_ref=dst.at[me], send_sem=ss.at[other], recv_sem=rs.at[me],
                device_id={axis: other}, device_id_type=pl.DeviceIdType.MESH,
            )

        def arrival(k):
            other = lax.rem(me + k, N)
            return pltpu.make_async_remote_copy(
                src_ref=src.at[other], dst_ref=dst.at[other], send_sem=ss.at[other], recv_sem=rs.at[other],
                device_id={axis: other}, device_id_type=pl.DeviceIdType.MESH,
            )

        def start():
            lax.fori_loop(1, N, lambda k, c: (copy(k).start(), c)[1], 0)

        def recv():
            lax.fori_loop(1, N, lambda k, c: (arrival(k).wait_recv(), c)[1], 0)

        def sent():
            lax.fori_loop(1, N, lambda k, c: (copy(k).wait_send(), c)[1], 0)

        return start, recv, sent

    loads[0].wait()
    for a in range(3):
        for lp in range(5):
            block = st[:, 8 * a : 8 * a + 8, 256 * lp : 256 * lp + 256]
            stacked = jnp.concatenate([block[:, :, :128], block[:, :, 128:]], axis=1)
            s_send[a * 5 + lp] = stacked.reshape(80, 128).astype(BF16)

    pl.semaphore_wait(barrier, 2 * (N - 1))

    def s_copy(other):
        return pltpu.make_async_remote_copy(
            src_ref=s_send.at[other], dst_ref=s_recv.at[g], send_sem=s_ss.at[other], recv_sem=s_rs.at[g],
            device_id={"grp": other}, device_id_type=pl.DeviceIdType.MESH,
        )

    def s_start(k, carry):
        other = lax.rem(g + k, N)

        @pl.when(other < TILES)
        def _():
            s_copy(other).start()

        return carry

    lax.fori_loop(1, N, s_start, 0)

    rows = st[...].reshape(C5 * LAT, NLON)
    west, east = rows[:, :HALF], rows[:, HALF:]
    pad = jnp.zeros((8, HALF), F32)
    even = jnp.concatenate([west + east, pad], 0).astype(BF16)
    odd = jnp.concatenate([west - east, pad], 0).astype(BF16)
    value = 2 * (lax.broadcasted_iota(jnp.int32, (256, 256), 0) % 128) + lax.broadcasted_iota(jnp.int32, (256, 256), 0) // 128
    hot = (value == pair_v[...]).astype(F32)
    for h in range(2):
        ohf[256 * h : 256 * h + 256, :] = hot[128 * h : 128 * h + 128, :].T
        oh[:, 128 * h : 128 * h + 128] = ohf[256 * h : 256 * h + 256, :].astype(BF16)
        for k in range(N):
            turned = ohf[pl.ds(256 * h + k, N, stride=N), :].astype(BF16)
            ohbg[k * N : (k + 1) * N, 128 * h : 128 * h + 128] = turned
    loads[1].wait()
    nt = (((1,), (1,)), ((), ()))
    nn = (((1,), (0,)), ((), ()))
    ce = lax.dot_general(tab[:512, :], even, nt, preferred_element_type=F32).astype(BF16)
    co = lax.dot_general(tab[512:, :], odd, nt, preferred_element_type=F32).astype(BF16)
    for j in range(4):
        e, o = ce[128 * j : 128 * j + 128], co[128 * j : 128 * j + 128]
        natural = jnp.concatenate([e, o] if j < 2 else [o, e], 0)
        slots = lax.dot_general(ohbg[...], natural, nn, preferred_element_type=F32).astype(BF16)
        f1_send[:, 16 * j : 16 * j + 16, :] = slots.reshape(N, 16, 128)

    f1_start, f1_wait, f1_sent = exchange("band", b, f1_send, f1_recv, f1_ss, f1_rs)
    f1_start()
    f1_recv[b] = f1_send[b]

    p = pair_s[g * N + b]
    loads[2].wait()
    legb[0:512, :] = leg[0:512, :].astype(BF16)
    last = jnp.where(
        lax.broadcasted_iota(jnp.int32, (16, 384), 0) == 0, jnp.broadcast_to(leg[512:513, :], (16, 384)), 0.0
    )
    legb[512:528, :] = last.astype(BF16)
    legt[:, 0:512] = leg[0:512, :].T.astype(BF16)
    legt[:, 512:528] = last.T.astype(BF16)
    lane = lax.broadcasted_iota(jnp.int32, (1, 384), 1)
    chan = (lane % N) * C5 + jnp.minimum(2 * (lane // 128) + (lane % 128) // 64, C5 - 1)
    damping = jnp.zeros((1, 384), F32)
    for k in range(80):
        damping = jnp.where(chan == k, diff_s[k], damping)
    row = lax.broadcasted_iota(jnp.int32, (ROWS, 384), 0)
    first = row < M - p
    degree = jnp.where(first, p + row, row - 1).astype(F32)
    scaled = degree * (degree + 1.0) / F32(M * (M + 1))
    low = (lane % 64) < 32
    weight = jnp.where(low & (p == 0), F32(1.0 / NLON), F32(2.0 / NLON))
    fac[...] = jnp.where(first == low, jnp.exp(-damping * scaled) * weight, 0.0)
    loads[3].wait()
    loads[4].wait()
    wint[...] = win[...].astype(F32).T.astype(BF16)
    woutt[...] = wout[...].astype(F32).T.astype(BF16)

    def relay(src, dst):
        mid[...] = src[...].reshape(1024, 128).astype(F32)
        for k in range(N):
            for j in range(4):
                dst[k, 16 * j : 16 * j + 16, :] = mid[pl.ds(16 * j + k, N, stride=64), :].astype(BF16)

    f1_wait()
    relay(f1_recv, f2_send)
    f2_start, f2_wait, f2_sent = exchange("grp", g, f2_send, f2_recv, f2_ss, f2_rs)
    f2_start()
    f2_recv[g] = f2_send[g]

    def t_copy(other):
        return pltpu.make_async_remote_copy(
            src_ref=t_send.at[other], dst_ref=t_recv.at[g], send_sem=t_ss.at[other], recv_sem=t_rs.at[g],
            device_id={"grp": other}, device_id_type=pl.DeviceIdType.MESH,
        )

    @pl.when(g < TILES)
    def _():
        s_recv[g] = s_send[g]

        def arrive(k, carry):
            other = lax.rem(g + k, N)
            pltpu.make_async_remote_copy(
                src_ref=s_send.at[0], dst_ref=s_recv.at[other], send_sem=s_ss.at[0], recv_sem=s_rs.at[other],
                device_id={"grp": other}, device_id_type=pl.DeviceIdType.MESH,
            ).wait_recv()
            return carry

        lax.fori_loop(1, N, arrive, 0)
        phys[...] = s_recv[...].reshape(1280, 128).astype(F32)
        for i in range(16):
            xb[:, 128 * i : 128 * i + 128] = phys[pl.ds(i, 80, stride=16), :].astype(BF16)
        for i in range(8):
            x = xb[:, 256 * i : 256 * i + 256]
            half = lax.dot_general(wint[...], x, nn, preferred_element_type=F32) * 0.5
            hidden = (half + half * jnp.tanh(half)).astype(BF16)
            tend = lax.dot_general(woutt[...], hidden, nn, preferred_element_type=F32)
            phys[pl.ds(2 * i, 80, stride=16), :] = tend[:, :128]
            phys[pl.ds(2 * i + 1, 80, stride=16), :] = tend[:, 128:]
        t_send[...] = phys[...].reshape(N, 80, 128).astype(BF16)

        def send(k, carry):
            other = lax.rem(g + k, N)
            t_copy(other).start()
            return carry

        lax.fori_loop(1, N, send, 0)
        t_recv[g] = t_send[g]

    f2_wait()
    mid[...] = f2_recv[...].reshape(1024, 128).astype(F32)
    left = lax.broadcasted_iota(jnp.int32, (LAT, 128), 1) < 64
    for k in range(N):
        part = jnp.concatenate([mid[pl.ds(16 * j + k, N, stride=64), :] for j in range(4)], 0)
        turned = jnp.concatenate([part, part], 0).T
        at = slice(LAT * k, LAT * k + LAT)
        zf[at, 0:128] = jnp.where(left, turned[0:24], turned[24:48])
        zf[at, 128:256] = jnp.where(left, turned[48:72], turned[72:96])
        zf[at, 256:384] = turned[96:120]
    proj = lax.dot_general(legb[...], zf[...].astype(BF16), nn, preferred_element_type=F32)
    spec = (proj * fac[...]).astype(BF16)
    zf[...] = lax.dot_general(legt[...], spec, nn, preferred_element_type=F32)
    lanes = lax.broadcasted_iota(jnp.int32, (64, 128), 1)
    odd_chan = ((lanes // LAT) % 2) == 1
    for k in range(N):
        at = slice(LAT * k, LAT * k + LAT)
        t0, t1, t2 = zf[at, 0:128], zf[at, 128:256], zf[at, 256:384]
        turned = jnp.concatenate([t0, t0, t1, t1, t2, jnp.zeros((8, 128), F32)], 0).T
        b1_send[k] = jnp.where(odd_chan, turned[64:128], turned[0:64]).astype(BF16)

    b1_start, b1_wait, b1_sent = exchange("band", b, b1_send, b1_recv, b1_ss, b1_rs)
    b1_start()
    b1_recv[b] = b1_send[b]
    b1_wait()
    relay(b1_recv, b2_send)
    b2_start, b2_wait, b2_sent = exchange("grp", g, b2_send, b2_recv, b2_ss, b2_rs)
    b2_start()
    b2_recv[g] = b2_send[g]

    def t_arrive(k, carry):
        other = lax.rem(g + k, N)

        @pl.when(other < TILES)
        def _():
            pltpu.make_async_remote_copy(
                src_ref=t_send.at[0], dst_ref=t_recv.at[other], send_sem=t_ss.at[0], recv_sem=t_rs.at[other],
                device_id={"grp": other}, device_id_type=pl.DeviceIdType.MESH,
            ).wait_recv()

        return carry

    lax.fori_loop(1, N, t_arrive, 0)
    for a in range(3):
        for lp in range(5):
            block = t_recv[a * 5 + lp].astype(F32).reshape(C5, 16, 128)
            out_ref[:, 8 * a : 8 * a + 8, 256 * lp : 256 * lp + 128] = block[:, 0:8]
            out_ref[:, 8 * a : 8 * a + 8, 256 * lp + 128 : 256 * lp + 256] = block[:, 8:16]

    b2_wait()
    natural = []
    for j in range(4):
        slots = b2_recv[:, 16 * j : 16 * j + 16, :].reshape(256, 128).astype(F32).T.astype(BF16)
        natural.append(lax.dot_general(slots, oh[...], nn, preferred_element_type=F32).astype(BF16))
    n0, n1, n2, n3 = natural
    even = jnp.concatenate([n0[:, :128], n1[:, :128], n2[:, 128:], n3[:, 128:]], 1)
    odd = jnp.concatenate([n0[:, 128:], n1[:, 128:], n2[:, :128], n3[:, :128]], 1)
    even = lax.dot_general(even, tab[:512, :], nn, preferred_element_type=F32)
    odd = lax.dot_general(odd, tab[512:, :], nn, preferred_element_type=F32)
    west = (even + odd)[:120].reshape(C5, LAT, HALF)
    east = (even - odd)[:120].reshape(C5, LAT, HALF)
    out_ref[:, :, :HALF] += west
    out_ref[:, :, HALF:] += east

    def s_sent(k, carry):
        other = lax.rem(g + k, N)

        @pl.when(other < TILES)
        def _():
            s_copy(other).wait_send()

        return carry

    lax.fori_loop(1, N, s_sent, 0)

    @pl.when(g < TILES)
    def _():
        lax.fori_loop(1, N, lambda k, c: (t_copy(lax.rem(g + k, N)).wait_send(), c)[1], 0)

    f1_sent()
    f2_sent()
    b1_sent()
    b2_sent()


def shards(state, pair_of_slot, legendre, diffusion, w_in, w_out):
    table = jnp.asarray(transform_table())
    hbm = pl.BlockSpec(memory_space=pl.ANY)
    smem = pl.BlockSpec(memory_space=pltpu.SMEM)
    vmem = pl.BlockSpec(memory_space=pltpu.VMEM)
    dma = pltpu.SemaphoreType.DMA
    message = pltpu.VMEM((N, 64, 128), BF16)
    block = pltpu.VMEM((N, 80, 128), BF16)
    return pl.pallas_call(
        kernel,
        out_shape=jax.ShapeDtypeStruct(state.shape, F32),
        in_specs=[hbm, smem, vmem, hbm, smem, hbm, hbm, hbm],
        out_specs=vmem,
        scratch_shapes=[
            pltpu.VMEM(state.shape, F32),
            pltpu.VMEM((1024, HALF), BF16),
            pltpu.VMEM((513, 384), F32),
            pltpu.VMEM((80, 1024), BF16),
            pltpu.VMEM((1024, 80), BF16),
            *[block] * 4,
            *[message] * 8,
            pltpu.VMEM((1024, 128), F32),
            pltpu.VMEM((1280, 128), F32),
            pltpu.VMEM((80, 2048), BF16),
            pltpu.VMEM((384, 384), F32),
            pltpu.VMEM((ROWS, 384), F32),
            pltpu.VMEM((ROWS, 384), BF16),
            pltpu.VMEM((384, ROWS), BF16),
            pltpu.VMEM((1024, 80), BF16),
            pltpu.VMEM((80, 1024), BF16),
            pltpu.VMEM((512, 128), F32),
            pltpu.VMEM((256, 256), BF16),
            pltpu.VMEM((256, 256), BF16),
            dma((5,)),
            *[dma((N,))] * 12,
        ],
        compiler_params=pltpu.CompilerParams(
            collective_id=0, has_side_effects=True, vmem_limit_bytes=40 * 1024 * 1024
        ),
        cost_estimate=pl.CostEstimate(flops=2_500_000_000, bytes_accessed=4_000_000, transcendentals=2_400_000),
    )(state, pair_of_slot, pair_of_slot.reshape(1, 256), legendre, diffusion, w_in, w_out, table)


def solution(mesh):
    return jax.shard_map(
        shards,
        mesh=mesh,
        in_specs=(P("grp", "band", None), P(), P(("grp", "band"), None, None), P(), P(), P()),
        out_specs=P("grp", "band", None),
        check_vma=False,
    )
```

```python
import math

import jax
import jax.numpy as jnp
import numpy as np
from jax import lax
from jax.experimental import pallas as pl
from jax.experimental.pallas import tpu as pltpu
from jax.sharding import PartitionSpec as P

NLON = 1280
HALF = NLON // 2
M = 512
C5 = 5
LAT = 24
N = 16
ROWS = 528
TILES = 15
F32 = jnp.float32
BF16 = jnp.bfloat16


def transform_table():
    q = np.arange(128)
    lon = np.arange(HALF)
    blocks = []
    for parity in (0, 1):
        for j in range(4):
            p = 2 * q + (parity if j < 2 else 1 - parity)
            m = p if j < 2 else M - 1 - p
            phase = 2.0 * np.pi * ((m[:, None] * lon[None, :]) % NLON) / NLON
            blocks.append(np.cos(phase) if j % 2 == 0 else -np.sin(phase))
    return np.concatenate(blocks, 0).astype(jnp.bfloat16)


def kernel(
    state_h, pair_s, pair_v, leg_h, diff_s, win_h, woutt_h, tab_h,
    out_ref,
    st, tab, leg, win, woutt,
    s_send, s_recv, t_send, t_recv,
    f1_send, f1_recv, f2_send, f2_recv,
    b1_send, b1_recv, b2_send, b2_recv,
    mid, phys, xb, zf, fac, legb, legt, wint, ohf, oh, ohbg,
    load_sem, s_ss, s_rs, t_ss, t_rs, f1_ss, f1_rs, f2_ss, f2_rs, b1_ss, b1_rs, b2_ss, b2_rs,
):
    g = lax.axis_index("grp")
    b = lax.axis_index("band")

    loads = [
        pltpu.make_async_copy(src, dst, load_sem.at[i])
        for i, (src, dst) in enumerate(
            [(state_h, st), (tab_h, tab), (leg_h, leg), (win_h, win), (woutt_h, woutt)]
        )
    ]
    for load in loads:
        load.start()

    barrier = pltpu.get_barrier_semaphore()

    def greet(k, carry):
        pl.semaphore_signal(barrier, inc=1, device_id={"grp": lax.rem(g + k, N)}, device_id_type=pl.DeviceIdType.MESH)
        pl.semaphore_signal(barrier, inc=1, device_id={"band": lax.rem(b + k, N)}, device_id_type=pl.DeviceIdType.MESH)
        return carry

    lax.fori_loop(1, N, greet, 0)

    def targets(axis):
        if axis == "grp":
            steps = sorted(((x, z) for x in range(2) for z in range(8)), key=lambda s: -(2 * s[0] + min(s[1], 8 - s[1])))
            return [lax.rem(g // 8 + x, 2) * 8 + lax.rem(g % 8 + z, 8) for x, z in steps[:-1]]
        steps = sorted(
            ((y, x, c) for y in range(4) for x in range(2) for c in range(2)),
            key=lambda s: -(2 * min(s[0], 4 - s[0]) + 2 * s[1] + s[2]),
        )
        return [
            lax.rem(b // 4 + y, 4) * 4 + lax.rem(b // 2 % 2 + x, 2) * 2 + lax.rem(b % 2 + c, 2) for y, x, c in steps[:-1]
        ]

    def message(axis, src, dst, ss, rs, other):
        return pltpu.make_async_remote_copy(
            src_ref=src.at[other], dst_ref=dst.at[{"grp": g, "band": b}[axis]], send_sem=ss, recv_sem=rs,
            device_id={axis: other}, device_id_type=pl.DeviceIdType.MESH,
        )

    def bulk(axis, src, dst, ss, rs, count):
        return pltpu.make_async_remote_copy(
            src_ref=src.at[pl.ds(0, count)], dst_ref=dst.at[pl.ds(0, count)], send_sem=ss, recv_sem=rs,
            device_id={axis: lax.rem({"grp": g, "band": b}[axis] + 1, N)}, device_id_type=pl.DeviceIdType.MESH,
        )

    def exchange(*refs):
        def start():
            for other in targets(refs[0]):
                message(*refs, other).start()

        return start, bulk(*refs, N - 1).wait_recv, bulk(*refs, N - 1).wait_send

    loads[0].wait()
    for a in range(3):
        for lp in range(5):
            block = st[:, 8 * a : 8 * a + 8, 256 * lp : 256 * lp + 256]
            stacked = jnp.concatenate([block[:, :, :128], block[:, :, 128:]], axis=1)
            s_send[a * 5 + lp] = stacked.reshape(80, 128).astype(BF16)

    rows = st[...].reshape(C5 * LAT, NLON)
    west, east = rows[:, :HALF], rows[:, HALF:]
    pad = jnp.zeros((8, HALF), F32)
    even = jnp.concatenate([west + east, pad], 0).astype(BF16)
    odd = jnp.concatenate([west - east, pad], 0).astype(BF16)
    value = 2 * (lax.broadcasted_iota(jnp.int32, (256, 256), 0) % 128) + lax.broadcasted_iota(jnp.int32, (256, 256), 0) // 128
    hot = (value == pair_v[...]).astype(F32)
    for h in range(2):
        ohf[256 * h : 256 * h + 256, :] = hot[128 * h : 128 * h + 128, :].T
        oh[:, 128 * h : 128 * h + 128] = ohf[256 * h : 256 * h + 256, :].astype(BF16)
        for k in range(N):
            turned = ohf[pl.ds(256 * h + k, N, stride=N), :].astype(BF16)
            ohbg[k * N : (k + 1) * N, 128 * h : 128 * h + 128] = turned
    loads[1].wait()
    nt = (((1,), (1,)), ((), ()))
    nn = (((1,), (0,)), ((), ()))
    ce = lax.dot_general(tab[:512, :], even, nt, preferred_element_type=F32).astype(BF16)
    co = lax.dot_general(tab[512:, :], odd, nt, preferred_element_type=F32).astype(BF16)
    for j in range(4):
        e, o = ce[128 * j : 128 * j + 128], co[128 * j : 128 * j + 128]
        natural = jnp.concatenate([e, o] if j < 2 else [o, e], 0)
        slots = lax.dot_general(ohbg[...], natural, nn, preferred_element_type=F32).astype(BF16)
        f1_send[:, 16 * j : 16 * j + 16, :] = slots.reshape(N, 16, 128)

    f1_start, f1_wait, f1_sent = exchange("band", f1_send, f1_recv, f1_ss, f1_rs)
    pl.semaphore_wait(barrier, 2 * (N - 1))
    f1_start()
    states = ("grp", s_send, s_recv, s_ss, s_rs)
    for other in targets("grp"):

        @pl.when(other < TILES)
        def _(other=other):
            message(*states, other).start()

    f1_recv[b] = f1_send[b]

    p = pair_s[g * N + b]
    loads[2].wait()
    legb[0:512, :] = leg[0:512].reshape(512, 384).astype(BF16)
    last = jnp.where(
        lax.broadcasted_iota(jnp.int32, (16, 384), 0) == 0, jnp.broadcast_to(leg[512], (16, 384)), 0.0
    )
    legb[512:528, :] = last.astype(BF16)
    legt[:, 0:512] = leg[0:512].reshape(512, 384).T.astype(BF16)
    legt[:, 512:528] = last.T.astype(BF16)
    lane = lax.broadcasted_iota(jnp.int32, (1, 384), 1)
    chan = (lane % N) * C5 + jnp.minimum(2 * (lane // 128) + (lane % 128) // 64, C5 - 1)
    damping = jnp.zeros((1, 384), F32)
    for k in range(80):
        damping = jnp.where(chan == k, diff_s[k], damping)
    row = lax.broadcasted_iota(jnp.int32, (ROWS, 384), 0)
    first = row < M - p
    degree = jnp.where(first, p + row, row - 1).astype(F32)
    scaled = degree * (degree + 1.0) / F32(M * (M + 1))
    low = (lane % 64) < 32
    weight = jnp.where(low & (p == 0), F32(1.0 / NLON), F32(2.0 / NLON))
    fac[...] = jnp.where(first == low, jnp.exp(-damping * scaled) * weight, 0.0)
    loads[3].wait()
    loads[4].wait()
    wint[...] = win[...].astype(F32).T.astype(BF16)

    def relay(src, dst):
        mid[...] = src[...].reshape(1024, 128).astype(F32)
        for k in range(N):
            for j in range(4):
                dst[k, 16 * j : 16 * j + 16, :] = mid[pl.ds(16 * j + k, N, stride=64), :].astype(BF16)

    f1_wait()
    relay(f1_recv, f2_send)
    f2_start, f2_wait, f2_sent = exchange("grp", f2_send, f2_recv, f2_ss, f2_rs)
    f2_start()
    f2_recv[g] = f2_send[g]

    tendencies = ("grp", t_send, t_recv, t_ss, t_rs)

    @pl.when(g < TILES)
    def _():
        s_recv[g] = s_send[g]
        bulk(*states, N - 1).wait_recv()
        phys[...] = s_recv[...].reshape(1280, 128).astype(F32)
        for i in range(16):
            xb[:, 128 * i : 128 * i + 128] = phys[pl.ds(i, 80, stride=16), :].astype(BF16)
        for i in range(8):
            x = xb[:, 256 * i : 256 * i + 256]
            half = lax.dot_general(wint[...], x, nn, preferred_element_type=F32) * 0.5
            hidden = (half + half * jnp.tanh(half)).astype(BF16)
            tend = lax.dot_general(woutt[...], hidden, nn, preferred_element_type=F32)
            phys[pl.ds(2 * i, 80, stride=16), :] = tend[:, :128]
            phys[pl.ds(2 * i + 1, 80, stride=16), :] = tend[:, 128:]
        t_send[...] = phys[...].reshape(N, 80, 128).astype(BF16)

        for other in targets("grp"):
            message(*tendencies, other).start()
        t_recv[g] = t_send[g]

    f1_sent()

    @pl.when(g < TILES)
    def _():
        bulk(*states, TILES - 1).wait_send()

    @pl.when(g >= TILES)
    def _():
        bulk(*states, TILES).wait_send()

    f2_wait()
    mid[...] = f2_recv[...].reshape(1024, 128).astype(F32)
    left = lax.broadcasted_iota(jnp.int32, (LAT, 128), 1) < 64
    for k in range(N):
        part = jnp.concatenate([mid[pl.ds(16 * j + k, N, stride=64), :] for j in range(4)], 0)
        turned = jnp.concatenate([part, part], 0).T
        at = slice(LAT * k, LAT * k + LAT)
        zf[at, 0:128] = jnp.where(left, turned[0:24], turned[24:48])
        zf[at, 128:256] = jnp.where(left, turned[48:72], turned[72:96])
        zf[at, 256:384] = turned[96:120]
    proj = lax.dot_general(legb[...], zf[...].astype(BF16), nn, preferred_element_type=F32)
    spec = (proj * fac[...]).astype(BF16)
    zf[...] = lax.dot_general(legt[...], spec, nn, preferred_element_type=F32)
    lanes = lax.broadcasted_iota(jnp.int32, (64, 128), 1)
    odd_chan = ((lanes // LAT) % 2) == 1
    for k in range(N):
        at = slice(LAT * k, LAT * k + LAT)
        t0, t1, t2 = zf[at, 0:128], zf[at, 128:256], zf[at, 256:384]
        turned = jnp.concatenate([t0, t0, t1, t1, t2, jnp.zeros((8, 128), F32)], 0).T
        b1_send[k] = jnp.where(odd_chan, turned[64:128], turned[0:64]).astype(BF16)

    b1_start, b1_wait, b1_sent = exchange("band", b1_send, b1_recv, b1_ss, b1_rs)
    b1_start()
    b1_recv[b] = b1_send[b]
    f2_sent()
    b1_wait()
    relay(b1_recv, b2_send)
    b2_start, b2_wait, b2_sent = exchange("grp", b2_send, b2_recv, b2_ss, b2_rs)
    b2_start()
    b2_recv[g] = b2_send[g]

    @pl.when(g < TILES)
    def _():
        bulk(*tendencies, TILES - 1).wait_recv()
        bulk(*tendencies, N - 1).wait_send()

    @pl.when(g >= TILES)
    def _():
        bulk(*tendencies, TILES).wait_recv()

    for a in range(3):
        for lp in range(5):
            block = t_recv[a * 5 + lp].astype(F32).reshape(C5, 16, 128)
            out_ref[:, 8 * a : 8 * a + 8, 256 * lp : 256 * lp + 128] = block[:, 0:8]
            out_ref[:, 8 * a : 8 * a + 8, 256 * lp + 128 : 256 * lp + 256] = block[:, 8:16]

    b1_sent()
    b2_wait()
    natural = []
    for j in range(4):
        slots = b2_recv[:, 16 * j : 16 * j + 16, :].reshape(256, 128).astype(F32).T.astype(BF16)
        natural.append(lax.dot_general(slots, oh[...], nn, preferred_element_type=F32).astype(BF16))
    n0, n1, n2, n3 = natural
    even = jnp.concatenate([n0[:, :128], n1[:, :128], n2[:, 128:], n3[:, 128:]], 1)
    odd = jnp.concatenate([n0[:, 128:], n1[:, 128:], n2[:, :128], n3[:, :128]], 1)
    even = lax.dot_general(even, tab[:512, :], nn, preferred_element_type=F32)
    odd = lax.dot_general(odd, tab[512:, :], nn, preferred_element_type=F32)
    west = (even + odd)[:120].reshape(C5, LAT, HALF)
    east = (even - odd)[:120].reshape(C5, LAT, HALF)
    out_ref[:, :, :HALF] += west
    out_ref[:, :, HALF:] += east

    b2_sent()


def shards(state, pair_of_slot, legendre, diffusion, w_in, w_out):
    table = jnp.asarray(transform_table())
    hbm = pl.BlockSpec(memory_space=pltpu.HBM)
    smem = pl.BlockSpec(memory_space=pltpu.SMEM)
    vmem = pl.BlockSpec(memory_space=pltpu.VMEM)
    dma = pltpu.SemaphoreType.DMA
    message = pltpu.VMEM((N, 64, 128), BF16)
    block = pltpu.VMEM((N, 80, 128), BF16)
    return pl.pallas_call(
        kernel,
        out_shape=jax.ShapeDtypeStruct(state.shape, F32),
        in_specs=[hbm, smem, vmem, hbm, smem, hbm, hbm, hbm],
        out_specs=vmem,
        scratch_shapes=[
            pltpu.VMEM(state.shape, F32),
            pltpu.VMEM((1024, HALF), BF16),
            pltpu.VMEM((513, 1, 384), F32),
            pltpu.VMEM((80, 1024), BF16),
            pltpu.VMEM((80, 1024), BF16),
            *[block] * 4,
            *[message] * 8,
            pltpu.VMEM((1024, 128), F32),
            pltpu.VMEM((1280, 128), F32),
            pltpu.VMEM((80, 2048), BF16),
            pltpu.VMEM((384, 384), F32),
            pltpu.VMEM((ROWS, 384), F32),
            pltpu.VMEM((ROWS, 384), BF16),
            pltpu.VMEM((384, ROWS), BF16),
            pltpu.VMEM((1024, 80), BF16),
            pltpu.VMEM((512, 128), F32),
            pltpu.VMEM((256, 256), BF16),
            pltpu.VMEM((256, 256), BF16),
            dma((5,)),
            *[dma] * 12,
        ],
        compiler_params=pltpu.CompilerParams(
            collective_id=0, has_side_effects=True, vmem_limit_bytes=56 * 1024 * 1024
        ),
        cost_estimate=pl.CostEstimate(flops=2_500_000_000, bytes_accessed=4_000_000, transcendentals=2_400_000),
    )(state, pair_of_slot, pair_of_slot.reshape(1, 256), jnp.swapaxes(legendre, 0, 1), diffusion, w_in, w_out.T, table)


def solution(mesh):
    return jax.shard_map(
        shards,
        mesh=mesh,
        in_specs=(P("grp", "band", None), P(), P(("grp", "band"), None, None), P(), P(), P()),
        out_specs=P("grp", "band", None),
        check_vma=False,
    )
```

```python
import math

import jax
import jax.numpy as jnp
import numpy as np
from jax import lax
from jax.experimental import pallas as pl
from jax.experimental.pallas import tpu as pltpu
from jax.sharding import PartitionSpec as P

NLON = 1280
HALF = NLON // 2
M = 512
C5 = 5
LAT = 24
N = 16
ROWS = 528
EARLY = 4
TILES = 15
F32 = jnp.float32
BF16 = jnp.bfloat16


def transform_table():
    q = np.arange(128)
    lon = np.arange(HALF)
    blocks = []
    for parity in (0, 1):
        for j in range(4):
            p = 2 * q + (parity if j < 2 else 1 - parity)
            m = p if j < 2 else M - 1 - p
            phase = 2.0 * np.pi * ((m[:, None] * lon[None, :]) % NLON) / NLON
            blocks.append(np.cos(phase) if j % 2 == 0 else -np.sin(phase))
    return np.concatenate(blocks, 0).astype(jnp.bfloat16)


def kernel(
    state_h, pair_h, pairv_h, leg_h, diff_h, win_h, woutt_h, tab_h,
    out_ref,
    st, tab, leg, win, woutt, pair_s, pair_v, diff_s,
    s_send, s_recv, t_send, t_recv,
    f1_send, f1_recv, f2_send, f2_recv, h1_send, h1_recv, h2_send, h2_recv,
    b1_send, b1_recv, b2_send, b2_recv, c1_send, c1_recv, c2_send, c2_recv,
    mid, mid2, phys, xb, zf, fac, legb, legt, wint, ohf, oh, ohbg,
    load_sem, s_ss, s_rs, t_ss, t_rs,
    f1_ss, f1_rs, f2_ss, f2_rs, h1_ss, h1_rs, h2_ss, h2_rs,
    b1_ss, b1_rs, b2_ss, b2_rs, c1_ss, c1_rs, c2_ss, c2_rs,
):
    g = lax.axis_index("grp")
    b = lax.axis_index("band")

    loads = [
        pltpu.make_async_copy(src, dst, load_sem.at[i])
        for i, (src, dst) in enumerate(
            [(state_h, st), (tab_h, tab), (leg_h, leg), (win_h, win), (woutt_h, woutt),
             (pair_h, pair_s), (pairv_h, pair_v), (diff_h, diff_s)]
        )
    ]
    for load in loads:
        load.start()

    barrier = pltpu.get_barrier_semaphore()

    def greet(k, carry):
        pl.semaphore_signal(barrier, inc=1, device_id={"grp": lax.rem(g + k, N)}, device_id_type=pl.DeviceIdType.MESH)
        pl.semaphore_signal(barrier, inc=1, device_id={"band": lax.rem(b + k, N)}, device_id_type=pl.DeviceIdType.MESH)
        return carry

    lax.fori_loop(1, N, greet, 0)

    def targets(axis):
        if axis == "grp":
            steps = sorted(((x, z) for x in range(2) for z in range(8)), key=lambda s: -(2 * s[0] + min(s[1], 8 - s[1])))
            return [lax.rem(g // 8 + x, 2) * 8 + lax.rem(g % 8 + z, 8) for x, z in steps[:-1]]
        steps = sorted(
            ((y, x, c) for y in range(4) for x in range(2) for c in range(2)),
            key=lambda s: -(2 * min(s[0], 4 - s[0]) + 2 * s[1] + s[2]),
        )
        return [
            lax.rem(b // 4 + y, 4) * 4 + lax.rem(b // 2 % 2 + x, 2) * 2 + lax.rem(b % 2 + c, 2) for y, x, c in steps[:-1]
        ]

    def message(axis, src, dst, ss, rs, other):
        return pltpu.make_async_remote_copy(
            src_ref=src.at[other], dst_ref=dst.at[{"grp": g, "band": b}[axis]], send_sem=ss, recv_sem=rs,
            device_id={axis: other}, device_id_type=pl.DeviceIdType.MESH,
        )

    def bulk(axis, src, dst, ss, rs, count):
        return pltpu.make_async_remote_copy(
            src_ref=src.at[pl.ds(0, count)], dst_ref=dst.at[pl.ds(0, count)], send_sem=ss, recv_sem=rs,
            device_id={axis: lax.rem({"grp": g, "band": b}[axis] + 1, N)}, device_id_type=pl.DeviceIdType.MESH,
        )

    def exchange(*refs):
        def start():
            for other in targets(refs[0]):
                message(*refs, other).start()

        return start, bulk(*refs, N - 1).wait_recv, bulk(*refs, N - 1).wait_send

    loads[0].wait()
    for a in range(3):
        for lp in range(5):
            block = st[:, 8 * a : 8 * a + 8, 256 * lp : 256 * lp + 256]
            stacked = jnp.concatenate([block[:, :, :128], block[:, :, 128:]], axis=1)
            s_send[a * 5 + lp] = stacked.reshape(80, 128).astype(BF16)

    rows = st[...].reshape(C5 * LAT, NLON)
    west, east = rows[:, :HALF], rows[:, HALF:]
    pad = jnp.zeros((8, HALF), F32)
    even = jnp.concatenate([west + east, pad], 0).astype(BF16)
    odd = jnp.concatenate([west - east, pad], 0).astype(BF16)
    value = 2 * (lax.broadcasted_iota(jnp.int32, (256, 256), 0) % 128) + lax.broadcasted_iota(jnp.int32, (256, 256), 0) // 128
    loads[6].wait()
    hot = (value == pair_v[...]).astype(F32)
    for h in range(2):
        ohf[256 * h : 256 * h + 256, :] = hot[128 * h : 128 * h + 128, :].T
        oh[:, 128 * h : 128 * h + 128] = ohf[256 * h : 256 * h + 256, :].astype(BF16)
        for k in range(N):
            turned = ohf[pl.ds(256 * h + k, N, stride=N), :].astype(BF16)
            ohbg[k * N : (k + 1) * N, 128 * h : 128 * h + 128] = turned
    loads[1].wait()
    nt = (((1,), (1,)), ((), ()))
    nn = (((1,), (0,)), ((), ()))
    ce = lax.dot_general(tab[:512, :], even, nt, preferred_element_type=F32).astype(BF16)
    co = lax.dot_general(tab[512:, :], odd, nt, preferred_element_type=F32).astype(BF16)
    for j in range(4):
        e, o = ce[128 * j : 128 * j + 128], co[128 * j : 128 * j + 128]
        natural = jnp.concatenate([e, o] if j < 2 else [o, e], 0)
        order, dst = (ohbg, f1_send) if j < 2 else (oh, h1_send)
        slots = lax.dot_general(order[...], natural, nn, preferred_element_type=F32).astype(BF16)
        dst[:, 16 * (j % 2) : 16 * (j % 2) + 16, :] = slots.reshape(N, 16, 128)

    f1_start, f1_wait, f1_sent = exchange("band", f1_send, f1_recv, f1_ss, f1_rs)
    f2_start, f2_wait, f2_sent = exchange("grp", f2_send, f2_recv, f2_ss, f2_rs)
    h1_start, h1_wait, h1_sent = exchange("grp", h1_send, h1_recv, h1_ss, h1_rs)
    h2_start, h2_wait, h2_sent = exchange("band", h2_send, h2_recv, h2_ss, h2_rs)
    pl.semaphore_wait(barrier, 2 * (N - 1))
    h1_start()
    f1_start()
    states = ("grp", s_send, s_recv, s_ss, s_rs)
    for other in targets("grp"):

        @pl.when(other < TILES)
        def _(other=other):
            message(*states, other).start()

    f1_recv[b] = f1_send[b]
    h1_recv[g] = h1_send[g]

    loads[5].wait()
    loads[7].wait()
    p = pair_s[g * N + b]
    loads[2].wait()
    legb[0:512, :] = leg[0:512].reshape(512, 384).astype(BF16)
    last = jnp.where(
        lax.broadcasted_iota(jnp.int32, (16, 384), 0) == 0, jnp.broadcast_to(leg[512], (16, 384)), 0.0
    )
    legb[512:528, :] = last.astype(BF16)
    legt[:, 0:512] = leg[0:512].reshape(512, 384).T.astype(BF16)
    legt[:, 512:528] = last.T.astype(BF16)
    lane = lax.broadcasted_iota(jnp.int32, (1, 384), 1)
    chan = (lane % N) * C5 + jnp.minimum(2 * (lane // 128) + (lane % 128) // 64, C5 - 1)
    damping = jnp.zeros((1, 384), F32)
    for k in range(80):
        damping = jnp.where(chan == k, diff_s[k], damping)
    row = lax.broadcasted_iota(jnp.int32, (ROWS, 384), 0)
    first = row < M - p
    degree = jnp.where(first, p + row, row - 1).astype(F32)
    scaled = degree * (degree + 1.0) / F32(M * (M + 1))
    low = (lane % 64) < 32
    weight = jnp.where(low & (p == 0), F32(1.0 / NLON), F32(2.0 / NLON))
    fac[...] = jnp.where(first == low, jnp.exp(-damping * scaled) * weight, 0.0)
    loads[3].wait()
    loads[4].wait()
    wint[...] = (win[...].astype(F32) * 0.5).T.astype(BF16)

    def relay(src, dst, mid):
        mid[...] = src[...].reshape(512, 128).astype(F32)
        for k in range(N):
            for j in range(2):
                dst[k, 16 * j : 16 * j + 16, :] = mid[pl.ds(16 * j + k, N, stride=32), :].astype(BF16)

    f1_wait()
    relay(f1_recv, f2_send, mid)
    f2_start()
    f2_recv[g] = f2_send[g]
    h1_wait()
    relay(h1_recv, h2_send, mid2)
    h2_start()
    h2_recv[b] = h2_send[b]

    tendencies = ("grp", t_send, t_recv, t_ss, t_rs)

    def column_tile(i):
        x = xb[:, 256 * i : 256 * i + 256]
        half = lax.dot_general(wint[...], x, nn, preferred_element_type=F32)
        hidden = (half + half * jnp.tanh(half)).astype(BF16)
        tend = lax.dot_general(woutt[...], hidden, nn, preferred_element_type=F32)
        phys[pl.ds(2 * i, 80, stride=16), :] = tend[:, :128]
        phys[pl.ds(2 * i + 1, 80, stride=16), :] = tend[:, 128:]

    @pl.when(g < TILES)
    def _():
        s_recv[g] = s_send[g]
        bulk(*states, N - 1).wait_recv()
        phys[...] = s_recv[...].reshape(1280, 128).astype(F32)
        for i in range(16):
            xb[:, 128 * i : 128 * i + 128] = phys[pl.ds(i, 80, stride=16), :].astype(BF16)
        for i in range(EARLY):
            column_tile(i)

    f1_sent()

    @pl.when(g < TILES)
    def _():
        bulk(*states, TILES - 1).wait_send()

    @pl.when(g >= TILES)
    def _():
        bulk(*states, TILES).wait_send()

    h1_sent()
    f2_wait()
    mid[...] = f2_recv[...].reshape(512, 128).astype(F32)
    h2_wait()
    left = lax.broadcasted_iota(jnp.int32, (LAT, 128), 1) < 64
    for k in range(N):
        part = jnp.concatenate([mid[pl.ds(16 * j + k, N, stride=32), :] for j in range(2)] + [h2_recv[k].astype(F32)], 0)
        turned = jnp.concatenate([part, part], 0).T
        at = slice(LAT * k, LAT * k + LAT)
        zf[at, 0:128] = jnp.where(left, turned[0:24], turned[24:48])
        zf[at, 128:256] = jnp.where(left, turned[48:72], turned[72:96])
        zf[at, 256:384] = turned[96:120]
    proj = lax.dot_general(legb[...], zf[...].astype(BF16), nn, preferred_element_type=F32)
    spec = (proj * fac[...]).astype(BF16)
    zf[...] = lax.dot_general(legt[...], spec, nn, preferred_element_type=F32)
    lanes = lax.broadcasted_iota(jnp.int32, (64, 128), 1)
    odd_chan = ((lanes // LAT) % 2) == 1
    for k in range(N):
        at = slice(LAT * k, LAT * k + LAT)
        t0, t1, t2 = zf[at, 0:128], zf[at, 128:256], zf[at, 256:384]
        turned = jnp.concatenate([t0, t0, t1, t1, t2, jnp.zeros((8, 128), F32)], 0).T
        turned = jnp.where(odd_chan, turned[64:128], turned[0:64])
        b1_send[k] = turned[0:32].astype(BF16)
        mid2[32 * k : 32 * k + 32, :] = turned[32:64]
    for k in range(N):
        for j in range(2):
            c1_send[k, 16 * j : 16 * j + 16, :] = mid2[pl.ds(16 * j + k, N, stride=32), :].astype(BF16)

    b1_start, b1_wait, b1_sent = exchange("band", b1_send, b1_recv, b1_ss, b1_rs)
    b2_start, b2_wait, b2_sent = exchange("grp", b2_send, b2_recv, b2_ss, b2_rs)
    c1_start, c1_wait, c1_sent = exchange("grp", c1_send, c1_recv, c1_ss, c1_rs)
    c2_start, c2_wait, c2_sent = exchange("band", c2_send, c2_recv, c2_ss, c2_rs)
    c1_start()
    b1_start()
    b1_recv[b] = b1_send[b]
    c1_recv[g] = c1_send[g]

    @pl.when(g < TILES)
    def _():
        for i in range(EARLY, 8):
            column_tile(i)
        t_send[...] = phys[...].reshape(N, 80, 128).astype(BF16)
        for other in targets("grp"):
            message(*tendencies, other).start()
        t_recv[g] = t_send[g]

    f2_sent()
    h2_sent()
    b1_wait()
    relay(b1_recv, b2_send, mid)
    b2_start()
    b2_recv[g] = b2_send[g]
    c1_wait()
    relay(c1_recv, c2_send, mid2)
    c2_start()
    c2_recv[b] = c2_send[b]

    @pl.when(g < TILES)
    def _():
        bulk(*tendencies, TILES - 1).wait_recv()
        bulk(*tendencies, N - 1).wait_send()

    @pl.when(g >= TILES)
    def _():
        bulk(*tendencies, TILES).wait_recv()

    for a in range(3):
        for lp in range(5):
            block = t_recv[a * 5 + lp].astype(F32).reshape(C5, 16, 128)
            out_ref[:, 8 * a : 8 * a + 8, 256 * lp : 256 * lp + 128] = block[:, 0:8]
            out_ref[:, 8 * a : 8 * a + 8, 256 * lp + 128 : 256 * lp + 256] = block[:, 8:16]

    b1_sent()
    c1_sent()
    b2_wait()
    c2_wait()
    natural = []
    for j in range(4):
        src, order = (b2_recv, oh) if j < 2 else (c2_recv, ohbg)
        at = 16 * (j % 2)
        slots = src[:, at : at + 16, :].reshape(256, 128).astype(F32).T.astype(BF16)
        natural.append(lax.dot_general(slots, order[...], nn, preferred_element_type=F32).astype(BF16))
    n0, n1, n2, n3 = natural
    even = jnp.concatenate([n0[:, :128], n1[:, :128], n2[:, 128:], n3[:, 128:]], 1)
    odd = jnp.concatenate([n0[:, 128:], n1[:, 128:], n2[:, :128], n3[:, :128]], 1)
    even = lax.dot_general(even, tab[:512, :], nn, preferred_element_type=F32)
    odd = lax.dot_general(odd, tab[512:, :], nn, preferred_element_type=F32)
    west = (even + odd)[:120].reshape(C5, LAT, HALF)
    east = (even - odd)[:120].reshape(C5, LAT, HALF)
    out_ref[:, :, :HALF] += west
    out_ref[:, :, HALF:] += east

    b2_sent()
    c2_sent()


def shards(state, pair_of_slot, legendre, diffusion, w_in, w_out):
    far = lambda x: pltpu.with_memory_space_constraint(x, pltpu.HBM)
    table = jnp.asarray(transform_table())
    hbm = pl.BlockSpec(memory_space=pltpu.HBM)
    vmem = pl.BlockSpec(memory_space=pltpu.VMEM)
    dma = pltpu.SemaphoreType.DMA
    message = pltpu.VMEM((N, 32, 128), BF16)
    block = pltpu.VMEM((N, 80, 128), BF16)
    return pl.pallas_call(
        kernel,
        out_shape=pltpu.VMEM(state.shape, F32),
        in_specs=[hbm] * 8,
        out_specs=vmem,
        scratch_shapes=[
            pltpu.VMEM(state.shape, F32),
            pltpu.VMEM((1024, HALF), BF16),
            pltpu.VMEM((513, 1, 384), F32),
            pltpu.VMEM((80, 1024), BF16),
            pltpu.VMEM((80, 1024), BF16),
            pltpu.SMEM((256,), jnp.int32),
            pltpu.VMEM((1, 256), jnp.int32),
            pltpu.SMEM((80,), F32),
            *[block] * 4,
            *[message] * 16,
            *[pltpu.VMEM((512, 128), F32)] * 2,
            pltpu.VMEM((1280, 128), F32),
            pltpu.VMEM((80, 2048), BF16),
            pltpu.VMEM((384, 384), F32),
            pltpu.VMEM((ROWS, 384), F32),
            pltpu.VMEM((ROWS, 384), BF16),
            pltpu.VMEM((384, ROWS), BF16),
            pltpu.VMEM((1024, 80), BF16),
            pltpu.VMEM((512, 128), F32),
            pltpu.VMEM((256, 256), BF16),
            pltpu.VMEM((256, 256), BF16),
            dma((8,)),
            *[dma] * 20,
        ],
        compiler_params=pltpu.CompilerParams(
            collective_id=0, has_side_effects=True, vmem_limit_bytes=40 * 1024 * 1024
        ),
        cost_estimate=pl.CostEstimate(flops=2_500_000_000, bytes_accessed=4_000_000, transcendentals=2_400_000),
    )(
        far(state), far(pair_of_slot), far(pair_of_slot.reshape(1, 256)), far(jnp.swapaxes(legendre, 0, 1)),
        far(diffusion), far(w_in), far(w_out.T), far(table)
    )


def solution(mesh):
    return jax.shard_map(
        shards,
        mesh=mesh,
        in_specs=(P("grp", "band", None), P(), P(("grp", "band"), None, None), P(), P(), P()),
        out_specs=P("grp", "band", None),
        check_vma=False,
    )
```

```python
import math

import jax
import jax.numpy as jnp
import numpy as np
from jax import lax
from jax.experimental import pallas as pl
from jax.experimental.pallas import tpu as pltpu
from jax.sharding import PartitionSpec as P

NLON = 1280
HALF = NLON // 2
M = 512
C5 = 5
LAT = 24
N = 16
ROWS = 528
TILES = 15
F32 = jnp.float32
BF16 = jnp.bfloat16


def transform_table():
    q = np.arange(128)
    lon = np.arange(HALF)
    blocks = []
    for parity in (0, 1):
        for j in range(4):
            p = 2 * q + (parity if j < 2 else 1 - parity)
            m = p if j < 2 else M - 1 - p
            phase = 2.0 * np.pi * ((m[:, None] * lon[None, :]) % NLON) / NLON
            blocks.append(np.cos(phase) if j % 2 == 0 else -np.sin(phase))
    return np.concatenate(blocks, 0).astype(jnp.bfloat16)


def kernel(
    state_h, pair_h, pairv_h, leg_h, diff_h, win_h, woutt_h, tab_h,
    out_ref,
    st, tab, leg, win, woutt, pair_s, pair_v, diff_s,
    s_send, s_recv, t_send, t_recv,
    f1_send, f1_recv, f2_send, f2_recv, h1_send, h1_recv, h2_send, h2_recv,
    b1_send, b1_recv, b2_send, b2_recv, c1_send, c1_recv, c2_send, c2_recv,
    mid, mid2, phys, phys2, xb, zf, fac, legb, legt, wint, ohf, oh, ohbg,
    load_sem, s_ss, s_rs, t_ss, t_rs, s2_ss, s2_rs, t2_ss, t2_rs,
    f1_ss, f1_rs, f2_ss, f2_rs, h1_ss, h1_rs, h2_ss, h2_rs,
    b1_ss, b1_rs, b2_ss, b2_rs, c1_ss, c1_rs, c2_ss, c2_rs,
):
    g = lax.axis_index("grp")
    b = lax.axis_index("band")

    loads = [
        pltpu.make_async_copy(src, dst, load_sem.at[i])
        for i, (src, dst) in enumerate(
            [(state_h, st), (tab_h, tab), (leg_h, leg), (win_h, win), (woutt_h, woutt),
             (pair_h, pair_s), (pairv_h, pair_v), (diff_h, diff_s)]
        )
    ]
    for load in loads:
        load.start()

    barrier = pltpu.get_barrier_semaphore()

    def greet(k, carry):
        pl.semaphore_signal(barrier, inc=1, device_id={"grp": lax.rem(g + k, N)}, device_id_type=pl.DeviceIdType.MESH)
        pl.semaphore_signal(barrier, inc=1, device_id={"band": lax.rem(b + k, N)}, device_id_type=pl.DeviceIdType.MESH)
        return carry

    lax.fori_loop(1, N, greet, 0)

    def targets(axis):
        if axis == "grp":
            steps = sorted(((x, z) for x in range(2) for z in range(8)), key=lambda s: -(2 * s[0] + min(s[1], 8 - s[1])))
            return [lax.rem(g // 8 + x, 2) * 8 + lax.rem(g % 8 + z, 8) for x, z in steps[:-1]]
        steps = sorted(
            ((y, x, c) for y in range(4) for x in range(2) for c in range(2)),
            key=lambda s: -(2 * min(s[0], 4 - s[0]) + 2 * s[1] + s[2]),
        )
        return [
            lax.rem(b // 4 + y, 4) * 4 + lax.rem(b // 2 % 2 + x, 2) * 2 + lax.rem(b % 2 + c, 2) for y, x, c in steps[:-1]
        ]

    def message(axis, src, dst, ss, rs, rows, other):
        return pltpu.make_async_remote_copy(
            src_ref=src.at[other, rows], dst_ref=dst.at[{"grp": g, "band": b}[axis], rows], send_sem=ss, recv_sem=rs,
            device_id={axis: other}, device_id_type=pl.DeviceIdType.MESH,
        )

    def bulk(axis, src, dst, ss, rs, rows, count):
        return pltpu.make_async_remote_copy(
            src_ref=src.at[pl.ds(0, count), rows], dst_ref=dst.at[pl.ds(0, count), rows], send_sem=ss, recv_sem=rs,
            device_id={axis: lax.rem({"grp": g, "band": b}[axis] + 1, N)}, device_id_type=pl.DeviceIdType.MESH,
        )

    def exchange(*refs):
        refs = (*refs, pl.ds(0, 32))

        def start():
            for other in targets(refs[0]):
                message(*refs, other).start()

        return start, bulk(*refs, N - 1).wait_recv, bulk(*refs, N - 1).wait_send

    loads[0].wait()
    for a in range(3):
        for lp in range(5):
            block = st[:, 8 * a : 8 * a + 8, 256 * lp : 256 * lp + 256]
            stacked = jnp.concatenate([block[:, :, :128], block[:, :, 128:]], axis=0)
            s_send[a * 5 + lp] = stacked.reshape(80, 128).astype(BF16)

    rows = st[...].reshape(C5 * LAT, NLON)
    west, east = rows[:, :HALF], rows[:, HALF:]
    pad = jnp.zeros((8, HALF), F32)
    even = jnp.concatenate([west + east, pad], 0).astype(BF16)
    odd = jnp.concatenate([west - east, pad], 0).astype(BF16)
    value = 2 * (lax.broadcasted_iota(jnp.int32, (256, 256), 0) % 128) + lax.broadcasted_iota(jnp.int32, (256, 256), 0) // 128
    loads[6].wait()
    hot = (value == pair_v[...]).astype(F32)
    for h in range(2):
        ohf[256 * h : 256 * h + 256, :] = hot[128 * h : 128 * h + 128, :].T
        oh[:, 128 * h : 128 * h + 128] = ohf[256 * h : 256 * h + 256, :].astype(BF16)
        for k in range(N):
            turned = ohf[pl.ds(256 * h + k, N, stride=N), :].astype(BF16)
            ohbg[k * N : (k + 1) * N, 128 * h : 128 * h + 128] = turned
    loads[1].wait()
    nt = (((1,), (1,)), ((), ()))
    nn = (((1,), (0,)), ((), ()))
    ce = lax.dot_general(tab[:512, :], even, nt, preferred_element_type=F32).astype(BF16)
    co = lax.dot_general(tab[512:, :], odd, nt, preferred_element_type=F32).astype(BF16)
    for j in range(4):
        e, o = ce[128 * j : 128 * j + 128], co[128 * j : 128 * j + 128]
        natural = jnp.concatenate([e, o] if j < 2 else [o, e], 0)
        order, dst = (ohbg, f1_send) if j < 2 else (oh, h1_send)
        slots = lax.dot_general(order[...], natural, nn, preferred_element_type=F32).astype(BF16)
        dst[:, 16 * (j % 2) : 16 * (j % 2) + 16, :] = slots.reshape(N, 16, 128)

    f1_start, f1_wait, f1_sent = exchange("band", f1_send, f1_recv, f1_ss, f1_rs)
    f2_start, f2_wait, f2_sent = exchange("grp", f2_send, f2_recv, f2_ss, f2_rs)
    h1_start, h1_wait, h1_sent = exchange("grp", h1_send, h1_recv, h1_ss, h1_rs)
    h2_start, h2_wait, h2_sent = exchange("band", h2_send, h2_recv, h2_ss, h2_rs)
    pl.semaphore_wait(barrier, 2 * (N - 1))
    h1_start()
    f1_start()
    states = ("grp", s_send, s_recv, s_ss, s_rs, pl.ds(0, 48))
    states2 = ("grp", s_send, s_recv, s2_ss, s2_rs, pl.ds(48, 32))

    def send_states(part):
        for other in targets("grp"):

            @pl.when(other < TILES)
            def _(other=other):
                message(*part, other).start()

    send_states(states)
    f1_recv[b] = f1_send[b]
    h1_recv[g] = h1_send[g]

    loads[5].wait()
    loads[7].wait()
    p = pair_s[g * N + b]
    loads[2].wait()
    legb[0:512, :] = leg[0:512].reshape(512, 384).astype(BF16)
    last = jnp.where(
        lax.broadcasted_iota(jnp.int32, (16, 384), 0) == 0, jnp.broadcast_to(leg[512], (16, 384)), 0.0
    )
    legb[512:528, :] = last.astype(BF16)
    legt[:, 0:512] = leg[0:512].reshape(512, 384).T.astype(BF16)
    legt[:, 512:528] = last.T.astype(BF16)
    lane = lax.broadcasted_iota(jnp.int32, (1, 384), 1)
    chan = (lane % N) * C5 + jnp.minimum(2 * (lane // 128) + (lane % 128) // 64, C5 - 1)
    damping = jnp.zeros((1, 384), F32)
    for k in range(80):
        damping = jnp.where(chan == k, diff_s[k], damping)
    row = lax.broadcasted_iota(jnp.int32, (ROWS, 384), 0)
    first = row < M - p
    degree = jnp.where(first, p + row, row - 1).astype(F32)
    scaled = degree * (degree + 1.0) / F32(M * (M + 1))
    low = (lane % 64) < 32
    weight = jnp.where(low & (p == 0), F32(1.0 / NLON), F32(2.0 / NLON))
    fac[...] = jnp.where(first == low, jnp.exp(-damping * scaled) * weight, 0.0)
    loads[3].wait()
    loads[4].wait()
    wint[...] = (win[...].astype(F32) * 0.5).T.astype(BF16)

    def relay(src, dst, mid):
        mid[...] = src[...].reshape(512, 128).astype(F32)
        for k in range(N):
            for j in range(2):
                dst[k, 16 * j : 16 * j + 16, :] = mid[pl.ds(16 * j + k, N, stride=32), :].astype(BF16)

    f1_wait()
    relay(f1_recv, f2_send, mid)
    f2_start()
    send_states(states2)
    f2_recv[g] = f2_send[g]
    h1_wait()
    relay(h1_recv, h2_send, mid2)
    h2_start()
    h2_recv[b] = h2_send[b]

    tendencies = ("grp", t_send, t_recv, t_ss, t_rs, pl.ds(0, 32))
    tendencies2 = ("grp", t_send, t_recv, t2_ss, t2_rs, pl.ds(32, 48))

    def column_half(buffer):
        for i in range(8):
            xb[:, 128 * i : 128 * i + 128] = buffer[pl.ds(i, 80, stride=8), :].astype(BF16)
        for i in range(4):
            x = xb[:, 256 * i : 256 * i + 256]
            half = lax.dot_general(wint[...], x, nn, preferred_element_type=F32)
            hidden = (half + half * jnp.tanh(half)).astype(BF16)
            tend = lax.dot_general(woutt[...], hidden, nn, preferred_element_type=F32)
            buffer[pl.ds(2 * i, 80, stride=8), :] = tend[:, :128]
            buffer[pl.ds(2 * i + 1, 80, stride=8), :] = tend[:, 128:]

    @pl.when(g < TILES)
    def _():
        s_recv[g] = s_send[g]
        bulk(*states, N - 1).wait_recv()
        phys[...] = s_recv[:, 0:48, :].astype(F32)[:, 0:40].reshape(640, 128)
        column_half(phys)
        t_send[:, 0:32, :] = phys[...].reshape(N, 40, 128)[:, 0:32].astype(BF16)
        for other in targets("grp"):
            message(*tendencies, other).start()

    f1_sent()

    @pl.when(g < TILES)
    def _():
        bulk(*states, TILES - 1).wait_send()
        bulk(*states2, TILES - 1).wait_send()

    @pl.when(g >= TILES)
    def _():
        bulk(*states, TILES).wait_send()
        bulk(*states2, TILES).wait_send()

    h1_sent()
    f2_wait()
    mid[...] = f2_recv[...].reshape(512, 128).astype(F32)
    h2_wait()
    left = lax.broadcasted_iota(jnp.int32, (LAT, 128), 1) < 64
    for k in range(N):
        part = jnp.concatenate([mid[pl.ds(16 * j + k, N, stride=32), :] for j in range(2)] + [h2_recv[k].astype(F32)], 0)
        turned = jnp.concatenate([part, part], 0).T
        at = slice(LAT * k, LAT * k + LAT)
        zf[at, 0:128] = jnp.where(left, turned[0:24], turned[24:48])
        zf[at, 128:256] = jnp.where(left, turned[48:72], turned[72:96])
        zf[at, 256:384] = turned[96:120]
    proj = lax.dot_general(legb[...], zf[...].astype(BF16), nn, preferred_element_type=F32)
    spec = (proj * fac[...]).astype(BF16)
    zf[...] = lax.dot_general(legt[...], spec, nn, preferred_element_type=F32)
    lanes = lax.broadcasted_iota(jnp.int32, (64, 128), 1)
    odd_chan = ((lanes // LAT) % 2) == 1
    for k in range(N):
        at = slice(LAT * k, LAT * k + LAT)
        t0, t1, t2 = zf[at, 0:128], zf[at, 128:256], zf[at, 256:384]
        turned = jnp.concatenate([t0, t0, t1, t1, t2, jnp.zeros((8, 128), F32)], 0).T
        turned = jnp.where(odd_chan, turned[64:128], turned[0:64])
        b1_send[k] = turned[0:32].astype(BF16)
        mid2[32 * k : 32 * k + 32, :] = turned[32:64]
    for k in range(N):
        for j in range(2):
            c1_send[k, 16 * j : 16 * j + 16, :] = mid2[pl.ds(16 * j + k, N, stride=32), :].astype(BF16)

    b1_start, b1_wait, b1_sent = exchange("band", b1_send, b1_recv, b1_ss, b1_rs)
    b2_start, b2_wait, b2_sent = exchange("grp", b2_send, b2_recv, b2_ss, b2_rs)
    c1_start, c1_wait, c1_sent = exchange("grp", c1_send, c1_recv, c1_ss, c1_rs)
    c2_start, c2_wait, c2_sent = exchange("band", c2_send, c2_recv, c2_ss, c2_rs)
    c1_start()
    b1_start()
    b1_recv[b] = b1_send[b]
    c1_recv[g] = c1_send[g]

    @pl.when(g < TILES)
    def _():
        bulk(*states2, N - 1).wait_recv()
        phys2[...] = s_recv[:, 32:80, :].astype(F32)[:, 8:48].reshape(640, 128)
        column_half(phys2)
        rest = jnp.concatenate([phys[...].reshape(N, 40, 128)[:, 32:40], phys2[...].reshape(N, 40, 128)], axis=1)
        t_send[:, 32:80, :] = rest.astype(BF16)
        for other in targets("grp"):
            message(*tendencies2, other).start()
        t_recv[g] = t_send[g]

    f2_sent()
    h2_sent()
    b1_wait()
    relay(b1_recv, b2_send, mid)
    b2_start()
    b2_recv[g] = b2_send[g]
    c1_wait()
    relay(c1_recv, c2_send, mid2)
    c2_start()
    c2_recv[b] = c2_send[b]

    @pl.when(g < TILES)
    def _():
        bulk(*tendencies, TILES - 1).wait_recv()
        bulk(*tendencies2, TILES - 1).wait_recv()
        bulk(*tendencies, N - 1).wait_send()
        bulk(*tendencies2, N - 1).wait_send()

    @pl.when(g >= TILES)
    def _():
        bulk(*tendencies, TILES).wait_recv()
        bulk(*tendencies2, TILES).wait_recv()

    for a in range(3):
        for lp in range(5):
            block = t_recv[a * 5 + lp].astype(F32)
            out_ref[:, 8 * a : 8 * a + 8, 256 * lp : 256 * lp + 128] = block[0:40].reshape(C5, 8, 128)
            out_ref[:, 8 * a : 8 * a + 8, 256 * lp + 128 : 256 * lp + 256] = block[40:80].reshape(C5, 8, 128)

    b1_sent()
    c1_sent()
    b2_wait()
    c2_wait()
    natural = []
    for j in range(4):
        src, order = (b2_recv, oh) if j < 2 else (c2_recv, ohbg)
        at = 16 * (j % 2)
        slots = src[:, at : at + 16, :].reshape(256, 128).astype(F32).T.astype(BF16)
        natural.append(lax.dot_general(slots, order[...], nn, preferred_element_type=F32).astype(BF16))
    n0, n1, n2, n3 = natural
    even = jnp.concatenate([n0[:, :128], n1[:, :128], n2[:, 128:], n3[:, 128:]], 1)
    odd = jnp.concatenate([n0[:, 128:], n1[:, 128:], n2[:, :128], n3[:, :128]], 1)
    even = lax.dot_general(even, tab[:512, :], nn, preferred_element_type=F32)
    odd = lax.dot_general(odd, tab[512:, :], nn, preferred_element_type=F32)
    west = (even + odd)[:120].reshape(C5, LAT, HALF)
    east = (even - odd)[:120].reshape(C5, LAT, HALF)
    out_ref[:, :, :HALF] += west
    out_ref[:, :, HALF:] += east

    b2_sent()
    c2_sent()


def shards(state, pair_of_slot, legendre, diffusion, w_in, w_out):
    far = lambda x: pltpu.with_memory_space_constraint(x, pltpu.HBM)
    table = jnp.asarray(transform_table())
    hbm = pl.BlockSpec(memory_space=pltpu.HBM)
    vmem = pl.BlockSpec(memory_space=pltpu.VMEM)
    dma = pltpu.SemaphoreType.DMA
    message = pltpu.VMEM((N, 32, 128), BF16)
    block = pltpu.VMEM((N, 80, 128), BF16)
    return pl.pallas_call(
        kernel,
        out_shape=pltpu.VMEM(state.shape, F32),
        in_specs=[hbm] * 8,
        out_specs=vmem,
        scratch_shapes=[
            pltpu.VMEM(state.shape, F32),
            pltpu.VMEM((1024, HALF), BF16),
            pltpu.VMEM((513, 1, 384), F32),
            pltpu.VMEM((80, 1024), BF16),
            pltpu.VMEM((80, 1024), BF16),
            pltpu.SMEM((256,), jnp.int32),
            pltpu.VMEM((1, 256), jnp.int32),
            pltpu.SMEM((80,), F32),
            *[block] * 4,
            *[message] * 16,
            *[pltpu.VMEM((512, 128), F32)] * 2,
            *[pltpu.VMEM((640, 128), F32)] * 2,
            pltpu.VMEM((80, 1024), BF16),
            pltpu.VMEM((384, 384), F32),
            pltpu.VMEM((ROWS, 384), F32),
            pltpu.VMEM((ROWS, 384), BF16),
            pltpu.VMEM((384, ROWS), BF16),
            pltpu.VMEM((1024, 80), BF16),
            pltpu.VMEM((512, 128), F32),
            pltpu.VMEM((256, 256), BF16),
            pltpu.VMEM((256, 256), BF16),
            dma((8,)),
            *[dma] * 24,
        ],
        compiler_params=pltpu.CompilerParams(
            collective_id=0, has_side_effects=True, vmem_limit_bytes=40 * 1024 * 1024
        ),
        cost_estimate=pl.CostEstimate(flops=2_500_000_000, bytes_accessed=4_000_000, transcendentals=2_400_000),
    )(
        far(state), far(pair_of_slot), far(pair_of_slot.reshape(1, 256)), far(jnp.swapaxes(legendre, 0, 1)),
        far(diffusion), far(w_in), far(w_out.T), far(table)
    )


def solution(mesh):
    return jax.shard_map(
        shards,
        mesh=mesh,
        in_specs=(P("grp", "band", None), P(), P(("grp", "band"), None, None), P(), P(), P()),
        out_specs=P("grp", "band", None),
        check_vma=False,
    )
```

```python
import math

import jax
import jax.numpy as jnp
import numpy as np
from jax import lax
from jax.experimental import pallas as pl
from jax.experimental.pallas import tpu as pltpu
from jax.sharding import PartitionSpec as P

NLON = 1280
HALF = NLON // 2
M = 512
C5 = 5
LAT = 24
N = 16
ROWS = 528
TILES = 15
F32 = jnp.float32
BF16 = jnp.bfloat16


def transform_table():
    q = np.arange(128)
    lon = np.arange(HALF)
    blocks = []
    for parity in (0, 1):
        for j in range(4):
            p = 2 * q + (parity if j < 2 else 1 - parity)
            m = p if j < 2 else M - 1 - p
            phase = 2.0 * np.pi * ((m[:, None] * lon[None, :]) % NLON) / NLON
            blocks.append(np.cos(phase) if j % 2 == 0 else -np.sin(phase))
    return np.concatenate(blocks, 0).astype(jnp.bfloat16)


def kernel(
    state_h, pair_h, pairv_h, leg_h, diff_h, win_h, woutt_h, tab_h,
    out_ref,
    st, tab, leg, win, woutt, pair_s, pair_v, diff_s,
    s_send, s_recv, t_send, t_recv,
    f1_send, f1_recv, f2_send, f2_recv, h1_send, h1_recv, h2_send, h2_recv,
    b1_send, b1_recv, b2_send, b2_recv, c1_send, c1_recv, c2_send, c2_recv,
    mid, mid2, phys, phys2, xb, zf, fac, legb, legt, wint, ohf, oh, ohbg,
    load_sem, s_ss, s_rs, t_ss, t_rs, s2_ss, s2_rs, t2_ss, t2_rs,
    f1_ss, f1_rs, f2_ss, f2_rs, h1_ss, h1_rs, h2_ss, h2_rs,
    b1_ss, b1_rs, b2_ss, b2_rs, c1_ss, c1_rs, c2_ss, c2_rs,
):
    g = lax.axis_index("grp")
    b = lax.axis_index("band")

    def targets(axis):
        if axis == "grp":
            steps = sorted(((x, z) for x in range(2) for z in range(8)), key=lambda s: -(2 * s[0] + min(s[1], 8 - s[1])))
            return [lax.rem(g // 8 + x, 2) * 8 + lax.rem(g % 8 + z, 8) for x, z in steps[:-1]]
        steps = sorted(
            ((y, x, c) for y in range(4) for x in range(2) for c in range(2)),
            key=lambda s: -(2 * min(s[0], 4 - s[0]) + 2 * s[1] + s[2]),
        )
        return [
            lax.rem(b // 4 + y, 4) * 4 + lax.rem(b // 2 % 2 + x, 2) * 2 + lax.rem(b % 2 + c, 2) for y, x, c in steps[:-1]
        ]

    barrier = pltpu.get_barrier_semaphore()
    for axis in ("grp", "band"):
        for other in targets(axis):
            pl.semaphore_signal(barrier, inc=1, device_id={axis: other}, device_id_type=pl.DeviceIdType.MESH)

    loads = [
        pltpu.make_async_copy(src, dst, load_sem.at[i])
        for i, (src, dst) in enumerate(
            [(state_h, st), (tab_h, tab), (leg_h, leg), (win_h, win), (woutt_h, woutt),
             (pair_h, pair_s), (pairv_h, pair_v), (diff_h, diff_s)]
        )
    ]
    for load in loads:
        load.start()

    def message(axis, src, dst, ss, rs, rows, other):
        return pltpu.make_async_remote_copy(
            src_ref=src.at[other, rows], dst_ref=dst.at[{"grp": g, "band": b}[axis], rows], send_sem=ss, recv_sem=rs,
            device_id={axis: other}, device_id_type=pl.DeviceIdType.MESH,
        )

    def bulk(axis, src, dst, ss, rs, rows, count):
        return pltpu.make_async_remote_copy(
            src_ref=src.at[pl.ds(0, count), rows], dst_ref=dst.at[pl.ds(0, count), rows], send_sem=ss, recv_sem=rs,
            device_id={axis: lax.rem({"grp": g, "band": b}[axis] + 1, N)}, device_id_type=pl.DeviceIdType.MESH,
        )

    def exchange(*refs):
        refs = (*refs, pl.ds(0, 32))

        def start():
            for other in targets(refs[0]):
                message(*refs, other).start()

        return start, bulk(*refs, N - 1).wait_recv, bulk(*refs, N - 1).wait_send

    loads[0].wait()
    for a in range(3):
        for lp in range(5):
            block = st[:, 8 * a : 8 * a + 8, 256 * lp : 256 * lp + 256]
            stacked = jnp.concatenate([block[:, :, :128], block[:, :, 128:]], axis=0)
            s_send[a * 5 + lp] = stacked.reshape(80, 128).astype(BF16)

    rows = st[...].reshape(C5 * LAT, NLON)
    west, east = rows[:, :HALF], rows[:, HALF:]
    pad = jnp.zeros((8, HALF), F32)
    even = jnp.concatenate([west + east, pad], 0).astype(BF16)
    odd = jnp.concatenate([west - east, pad], 0).astype(BF16)
    value = 2 * (lax.broadcasted_iota(jnp.int32, (256, 256), 0) % 128) + lax.broadcasted_iota(jnp.int32, (256, 256), 0) // 128
    loads[6].wait()
    hot = (value == pair_v[...]).astype(F32)
    for h in range(2):
        ohf[256 * h : 256 * h + 256, :] = hot[128 * h : 128 * h + 128, :].T
        oh[:, 128 * h : 128 * h + 128] = ohf[256 * h : 256 * h + 256, :].astype(BF16)
        for k in range(N):
            turned = ohf[pl.ds(256 * h + k, N, stride=N), :].astype(BF16)
            ohbg[k * N : (k + 1) * N, 128 * h : 128 * h + 128] = turned
    loads[1].wait()
    nt = (((1,), (1,)), ((), ()))
    nn = (((1,), (0,)), ((), ()))
    ce = lax.dot_general(tab[:512, :], even, nt, preferred_element_type=F32).astype(BF16)
    co = lax.dot_general(tab[512:, :], odd, nt, preferred_element_type=F32).astype(BF16)
    for j in range(4):
        e, o = ce[128 * j : 128 * j + 128], co[128 * j : 128 * j + 128]
        natural = jnp.concatenate([e, o] if j < 2 else [o, e], 0)
        order, dst = (ohbg, f1_send) if j < 2 else (oh, h1_send)
        slots = lax.dot_general(order[...], natural, nn, preferred_element_type=F32).astype(BF16)
        dst[:, 16 * (j % 2) : 16 * (j % 2) + 16, :] = slots.reshape(N, 16, 128)

    f1_start, f1_wait, f1_sent = exchange("band", f1_send, f1_recv, f1_ss, f1_rs)
    f2_start, f2_wait, f2_sent = exchange("grp", f2_send, f2_recv, f2_ss, f2_rs)
    h1_start, h1_wait, h1_sent = exchange("grp", h1_send, h1_recv, h1_ss, h1_rs)
    h2_start, h2_wait, h2_sent = exchange("band", h2_send, h2_recv, h2_ss, h2_rs)
    pl.semaphore_wait(barrier, 2 * (N - 1))
    h1_start()
    f1_start()
    states = ("grp", s_send, s_recv, s_ss, s_rs, pl.ds(0, 48))
    states2 = ("grp", s_send, s_recv, s2_ss, s2_rs, pl.ds(48, 32))

    def send_states(part):
        for other in targets("grp"):

            @pl.when(other < TILES)
            def _(other=other):
                message(*part, other).start()

    send_states(states)
    f1_recv[b] = f1_send[b]
    h1_recv[g] = h1_send[g]

    loads[5].wait()
    loads[7].wait()
    p = pair_s[g * N + b]
    loads[2].wait()
    legb[0:512, :] = leg[0:512].reshape(512, 384).astype(BF16)
    last = jnp.where(
        lax.broadcasted_iota(jnp.int32, (16, 384), 0) == 0, jnp.broadcast_to(leg[512], (16, 384)), 0.0
    )
    legb[512:528, :] = last.astype(BF16)
    legt[:, 0:512] = leg[0:512].reshape(512, 384).T.astype(BF16)
    legt[:, 512:528] = last.T.astype(BF16)
    lane = lax.broadcasted_iota(jnp.int32, (1, 384), 1)
    chan = (lane % N) * C5 + jnp.minimum(2 * (lane // 128) + (lane % 128) // 64, C5 - 1)
    damping = jnp.zeros((1, 384), F32)
    for k in range(80):
        damping = jnp.where(chan == k, diff_s[k], damping)
    row = lax.broadcasted_iota(jnp.int32, (ROWS, 384), 0)
    first = row < M - p
    degree = jnp.where(first, p + row, row - 1).astype(F32)
    scaled = degree * (degree + 1.0) / F32(M * (M + 1))
    low = (lane % 64) < 32
    weight = jnp.where(low & (p == 0), F32(1.0 / NLON), F32(2.0 / NLON))
    fac[...] = jnp.where(first == low, jnp.exp(-damping * scaled) * weight, 0.0)
    loads[3].wait()
    loads[4].wait()
    wint[...] = (win[...].astype(F32) * 0.5).T.astype(BF16)

    def relay(src, dst, mid):
        mid[...] = src[...].reshape(512, 128).astype(F32)
        for k in range(N):
            for j in range(2):
                dst[k, 16 * j : 16 * j + 16, :] = mid[pl.ds(16 * j + k, N, stride=32), :].astype(BF16)

    f1_wait()
    relay(f1_recv, f2_send, mid)
    f2_start()
    send_states(states2)
    f2_recv[g] = f2_send[g]
    h1_wait()
    relay(h1_recv, h2_send, mid2)
    h2_start()
    h2_recv[b] = h2_send[b]

    tendencies = ("grp", t_send, t_recv, t_ss, t_rs, pl.ds(0, 32))
    tendencies2 = ("grp", t_send, t_recv, t2_ss, t2_rs, pl.ds(32, 48))

    def column_half(buffer):
        for i in range(8):
            xb[:, 128 * i : 128 * i + 128] = buffer[pl.ds(i, 80, stride=8), :].astype(BF16)
        half = lax.dot_general(wint[...], xb[...], nn, preferred_element_type=F32)
        hidden = (half + half * jnp.tanh(half)).astype(BF16)
        tend = lax.dot_general(woutt[...], hidden, nn, preferred_element_type=F32)
        for i in range(8):
            buffer[pl.ds(i, 80, stride=8), :] = tend[:, 128 * i : 128 * i + 128]

    @pl.when(g < TILES)
    def _():
        s_recv[g] = s_send[g]
        bulk(*states, N - 1).wait_recv()
        phys[...] = s_recv[:, 0:48, :].astype(F32)[:, 0:40].reshape(640, 128)
        column_half(phys)
        t_send[:, 0:32, :] = phys[...].reshape(N, 40, 128)[:, 0:32].astype(BF16)
        for other in reversed(targets("grp")):
            message(*tendencies, other).start()

    f1_sent()

    @pl.when(g < TILES)
    def _():
        bulk(*states, TILES - 1).wait_send()
        bulk(*states2, TILES - 1).wait_send()

    @pl.when(g >= TILES)
    def _():
        bulk(*states, TILES).wait_send()
        bulk(*states2, TILES).wait_send()

    h1_sent()
    f2_wait()
    mid[...] = f2_recv[...].reshape(512, 128).astype(F32)
    h2_wait()
    left = lax.broadcasted_iota(jnp.int32, (LAT, 128), 1) < 64
    for k in range(N):
        part = jnp.concatenate([mid[pl.ds(16 * j + k, N, stride=32), :] for j in range(2)] + [h2_recv[k].astype(F32)], 0)
        turned = jnp.concatenate([part, part], 0).T
        at = slice(LAT * k, LAT * k + LAT)
        zf[at, 0:128] = jnp.where(left, turned[0:24], turned[24:48])
        zf[at, 128:256] = jnp.where(left, turned[48:72], turned[72:96])
        zf[at, 256:384] = turned[96:120]
    proj = lax.dot_general(legb[...], zf[...].astype(BF16), nn, preferred_element_type=F32)
    spec = (proj * fac[...]).astype(BF16)
    zf[...] = lax.dot_general(legt[...], spec, nn, preferred_element_type=F32)
    lanes = lax.broadcasted_iota(jnp.int32, (64, 128), 1)
    odd_chan = ((lanes // LAT) % 2) == 1
    for k in range(N):
        at = slice(LAT * k, LAT * k + LAT)
        t0, t1, t2 = zf[at, 0:128], zf[at, 128:256], zf[at, 256:384]
        turned = jnp.concatenate([t0, t0, t1, t1, t2, jnp.zeros((8, 128), F32)], 0).T
        turned = jnp.where(odd_chan, turned[64:128], turned[0:64])
        b1_send[k] = turned[0:32].astype(BF16)
        mid2[32 * k : 32 * k + 32, :] = turned[32:64]
    for k in range(N):
        for j in range(2):
            c1_send[k, 16 * j : 16 * j + 16, :] = mid2[pl.ds(16 * j + k, N, stride=32), :].astype(BF16)

    b1_start, b1_wait, b1_sent = exchange("band", b1_send, b1_recv, b1_ss, b1_rs)
    b2_start, b2_wait, b2_sent = exchange("grp", b2_send, b2_recv, b2_ss, b2_rs)
    c1_start, c1_wait, c1_sent = exchange("grp", c1_send, c1_recv, c1_ss, c1_rs)
    c2_start, c2_wait, c2_sent = exchange("band", c2_send, c2_recv, c2_ss, c2_rs)
    c1_start()
    b1_start()
    b1_recv[b] = b1_send[b]
    c1_recv[g] = c1_send[g]

    @pl.when(g < TILES)
    def _():
        bulk(*states2, N - 1).wait_recv()
        phys2[...] = s_recv[:, 32:80, :].astype(F32)[:, 8:48].reshape(640, 128)
        column_half(phys2)
        rest = jnp.concatenate([phys[...].reshape(N, 40, 128)[:, 32:40], phys2[...].reshape(N, 40, 128)], axis=1)
        t_send[:, 32:80, :] = rest.astype(BF16)
        for other in reversed(targets("grp")):
            message(*tendencies2, other).start()
        t_recv[g] = t_send[g]

    f2_sent()
    h2_sent()
    b1_wait()
    relay(b1_recv, b2_send, mid)
    b2_start()
    b2_recv[g] = b2_send[g]
    c1_wait()
    relay(c1_recv, c2_send, mid2)
    c2_start()
    c2_recv[b] = c2_send[b]

    @pl.when(g < TILES)
    def _():
        bulk(*tendencies, TILES - 1).wait_recv()
        bulk(*tendencies2, TILES - 1).wait_recv()
        bulk(*tendencies, N - 1).wait_send()
        bulk(*tendencies2, N - 1).wait_send()

    @pl.when(g >= TILES)
    def _():
        bulk(*tendencies, TILES).wait_recv()
        bulk(*tendencies2, TILES).wait_recv()

    for a in range(3):
        for lp in range(5):
            block = t_recv[a * 5 + lp].astype(F32)
            out_ref[:, 8 * a : 8 * a + 8, 256 * lp : 256 * lp + 128] = block[0:40].reshape(C5, 8, 128)
            out_ref[:, 8 * a : 8 * a + 8, 256 * lp + 128 : 256 * lp + 256] = block[40:80].reshape(C5, 8, 128)

    b1_sent()
    c1_sent()
    b2_wait()
    c2_wait()
    natural = []
    for j in range(4):
        src, order = (b2_recv, oh) if j < 2 else (c2_recv, ohbg)
        at = 16 * (j % 2)
        slots = src[:, at : at + 16, :].reshape(256, 128).astype(F32).T.astype(BF16)
        natural.append(lax.dot_general(slots, order[...], nn, preferred_element_type=F32).astype(BF16))
    n0, n1, n2, n3 = natural
    even = jnp.concatenate([n0[:, :128], n1[:, :128], n2[:, 128:], n3[:, 128:]], 1)
    odd = jnp.concatenate([n0[:, 128:], n1[:, 128:], n2[:, :128], n3[:, :128]], 1)
    even = lax.dot_general(even, tab[:512, :], nn, preferred_element_type=F32)
    odd = lax.dot_general(odd, tab[512:, :], nn, preferred_element_type=F32)
    west = (even + odd)[:120].reshape(C5, LAT, HALF)
    east = (even - odd)[:120].reshape(C5, LAT, HALF)
    out_ref[:, :, :HALF] += west
    out_ref[:, :, HALF:] += east

    b2_sent()
    c2_sent()


def shards(state, pair_of_slot, legendre, diffusion, w_in, w_out):
    far = lambda x: pltpu.with_memory_space_constraint(x, pltpu.HBM)
    table = jnp.asarray(transform_table())
    hbm = pl.BlockSpec(memory_space=pltpu.HBM)
    vmem = pl.BlockSpec(memory_space=pltpu.VMEM)
    dma = pltpu.SemaphoreType.DMA
    message = pltpu.VMEM((N, 32, 128), BF16)
    block = pltpu.VMEM((N, 80, 128), BF16)
    return pl.pallas_call(
        kernel,
        out_shape=pltpu.VMEM(state.shape, F32),
        in_specs=[hbm] * 8,
        out_specs=vmem,
        scratch_shapes=[
            pltpu.VMEM(state.shape, F32),
            pltpu.VMEM((1024, HALF), BF16),
            pltpu.VMEM((513, 1, 384), F32),
            pltpu.VMEM((80, 1024), BF16),
            pltpu.VMEM((80, 1024), BF16),
            pltpu.SMEM((256,), jnp.int32),
            pltpu.VMEM((1, 256), jnp.int32),
            pltpu.SMEM((80,), F32),
            *[block] * 4,
            *[message] * 16,
            *[pltpu.VMEM((512, 128), F32)] * 2,
            *[pltpu.VMEM((640, 128), F32)] * 2,
            pltpu.VMEM((80, 1024), BF16),
            pltpu.VMEM((384, 384), F32),
            pltpu.VMEM((ROWS, 384), F32),
            pltpu.VMEM((ROWS, 384), BF16),
            pltpu.VMEM((384, ROWS), BF16),
            pltpu.VMEM((1024, 80), BF16),
            pltpu.VMEM((512, 128), F32),
            pltpu.VMEM((256, 256), BF16),
            pltpu.VMEM((256, 256), BF16),
            dma((8,)),
            *[dma] * 24,
        ],
        compiler_params=pltpu.CompilerParams(
            collective_id=0, has_side_effects=True, vmem_limit_bytes=40 * 1024 * 1024
        ),
        cost_estimate=pl.CostEstimate(flops=2_500_000_000, bytes_accessed=4_000_000, transcendentals=2_400_000),
    )(
        far(state), far(pair_of_slot), far(pair_of_slot.reshape(1, 256)), far(jnp.swapaxes(legendre, 0, 1)),
        far(diffusion), far(w_in), far(w_out.T), far(table)
    )


def solution(mesh):
    return jax.shard_map(
        shards,
        mesh=mesh,
        in_specs=(P("grp", "band", None), P(), P(("grp", "band"), None, None), P(), P(), P()),
        out_specs=P("grp", "band", None),
        check_vma=False,
    )
```

```python
import math

import jax
import jax.numpy as jnp
import numpy as np
from jax import lax
from jax.experimental import pallas as pl
from jax.experimental.pallas import tpu as pltpu
from jax.sharding import PartitionSpec as P

NLON = 1280
HALF = NLON // 2
M = 512
C5 = 5
LAT = 24
N = 16
ROWS = 528
TILES = 15
F32 = jnp.float32
BF16 = jnp.bfloat16


def transform_table():
    q = np.arange(128)
    lon = np.arange(HALF)
    blocks = []
    for parity in (0, 1):
        for j in range(4):
            p = 2 * q + (parity if j < 2 else 1 - parity)
            m = p if j < 2 else M - 1 - p
            phase = 2.0 * np.pi * ((m[:, None] * lon[None, :]) % NLON) / NLON
            blocks.append(np.cos(phase) if j % 2 == 0 else -np.sin(phase))
    return np.concatenate(blocks, 0).astype(jnp.bfloat16)


def kernel(
    state_h, pair_h, pairv_h, leg_h, diff_h, win_h, woutt_h, tab_h,
    out_ref,
    st, tab, leg, win, woutt, pair_s, pair_v, diff_s,
    s_send, s_recv, t_send, t_recv,
    f1_send, f1_recv, f2_send, f2_recv, h1_send, h1_recv, h2_send, h2_recv,
    b1_send, b1_recv, b2_send, b2_recv, c1_send, c1_recv, c2_send, c2_recv,
    mid, mid2, phys, phys2, xb, zf, fac, legb, legt, wint, ohf, oh, ohbg,
    load_sem, s_ss, s_rs, t_ss, t_rs, s2_ss, s2_rs, t2_ss, t2_rs,
    f1_ss, f1_rs, f2_ss, f2_rs, h1_ss, h1_rs, h2_ss, h2_rs,
    b1_ss, b1_rs, b2_ss, b2_rs, c1_ss, c1_rs, c2_ss, c2_rs,
):
    g = lax.axis_index("grp")
    b = lax.axis_index("band")

    def targets(axis):
        if axis == "grp":
            steps = sorted(((x, z) for x in range(2) for z in range(8)), key=lambda s: -(2 * s[0] + min(s[1], 8 - s[1])))
            return [lax.rem(g // 8 + x, 2) * 8 + lax.rem(g % 8 + z, 8) for x, z in steps[:-1]]
        steps = sorted(
            ((y, x, c) for y in range(4) for x in range(2) for c in range(2)),
            key=lambda s: -(2 * min(s[0], 4 - s[0]) + 2 * s[1] + s[2]),
        )
        return [
            lax.rem(b // 4 + y, 4) * 4 + lax.rem(b // 2 % 2 + x, 2) * 2 + lax.rem(b % 2 + c, 2) for y, x, c in steps[:-1]
        ]

    barrier = pltpu.get_barrier_semaphore()
    for axis in ("grp", "band"):
        for other in targets(axis):
            pl.semaphore_signal(barrier, inc=1, device_id={axis: other}, device_id_type=pl.DeviceIdType.MESH)

    loads = [
        pltpu.make_async_copy(src, dst, load_sem.at[i])
        for i, (src, dst) in enumerate(
            [(state_h, st), (tab_h, tab), (leg_h, leg), (win_h, win), (woutt_h, woutt),
             (pair_h, pair_s), (pairv_h, pair_v), (diff_h, diff_s)]
        )
    ]
    for load in loads:
        load.start()

    def message(axis, src, dst, ss, rs, rows, other):
        return pltpu.make_async_remote_copy(
            src_ref=src.at[other, rows], dst_ref=dst.at[{"grp": g, "band": b}[axis], rows], send_sem=ss, recv_sem=rs,
            device_id={axis: other}, device_id_type=pl.DeviceIdType.MESH,
        )

    def bulk(axis, src, dst, ss, rs, rows, count):
        return pltpu.make_async_remote_copy(
            src_ref=src.at[pl.ds(0, count), rows], dst_ref=dst.at[pl.ds(0, count), rows], send_sem=ss, recv_sem=rs,
            device_id={axis: lax.rem({"grp": g, "band": b}[axis] + 1, N)}, device_id_type=pl.DeviceIdType.MESH,
        )

    def exchange(*refs):
        refs = (*refs, pl.ds(0, 32))

        def start():
            for other in targets(refs[0]):
                message(*refs, other).start()

        return start, bulk(*refs, N - 1).wait_recv, bulk(*refs, N - 1).wait_send

    loads[0].wait()
    for a in range(3):
        for lp in range(5):
            block = st[:, 8 * a : 8 * a + 8, 256 * lp : 256 * lp + 256]
            stacked = jnp.concatenate([block[:, :, :128], block[:, :, 128:]], axis=0)
            s_send[a * 5 + lp] = stacked.reshape(80, 128).astype(BF16)

    rows = st[...].reshape(C5 * LAT, NLON)
    west, east = rows[:, :HALF], rows[:, HALF:]
    pad = jnp.zeros((8, HALF), F32)

    def terms(value):
        value = jnp.concatenate([value, pad], 0)
        high = value.astype(BF16)
        return jnp.concatenate([high, (value - high.astype(F32)).astype(BF16)], 0)

    even, odd = terms(west + east), terms(west - east)
    value = 2 * (lax.broadcasted_iota(jnp.int32, (256, 256), 0) % 128) + lax.broadcasted_iota(jnp.int32, (256, 256), 0) // 128
    loads[6].wait()
    hot = (value == pair_v[...]).astype(F32)
    for h in range(2):
        ohf[256 * h : 256 * h + 256, :] = hot[128 * h : 128 * h + 128, :].T
        oh[:, 128 * h : 128 * h + 128] = ohf[256 * h : 256 * h + 256, :].astype(BF16)
        for k in range(N):
            turned = ohf[pl.ds(256 * h + k, N, stride=N), :].astype(BF16)
            ohbg[k * N : (k + 1) * N, 128 * h : 128 * h + 128] = turned
    loads[1].wait()
    nt = (((1,), (1,)), ((), ()))
    nn = (((1,), (0,)), ((), ()))
    ce = lax.dot_general(tab[:512, :], even, nt, preferred_element_type=F32)
    co = lax.dot_general(tab[512:, :], odd, nt, preferred_element_type=F32)
    ce = (ce[:, :128] + ce[:, 128:]).astype(BF16)
    co = (co[:, :128] + co[:, 128:]).astype(BF16)
    for j in range(4):
        e, o = ce[128 * j : 128 * j + 128], co[128 * j : 128 * j + 128]
        natural = jnp.concatenate([e, o] if j < 2 else [o, e], 0)
        order, dst = (ohbg, f1_send) if j < 2 else (oh, h1_send)
        slots = lax.dot_general(order[...], natural, nn, preferred_element_type=F32).astype(BF16)
        dst[:, 16 * (j % 2) : 16 * (j % 2) + 16, :] = slots.reshape(N, 16, 128)

    f1_start, f1_wait, f1_sent = exchange("band", f1_send, f1_recv, f1_ss, f1_rs)
    f2_start, f2_wait, f2_sent = exchange("grp", f2_send, f2_recv, f2_ss, f2_rs)
    h1_start, h1_wait, h1_sent = exchange("grp", h1_send, h1_recv, h1_ss, h1_rs)
    h2_start, h2_wait, h2_sent = exchange("band", h2_send, h2_recv, h2_ss, h2_rs)
    pl.semaphore_wait(barrier, 2 * (N - 1))
    h1_start()
    f1_start()
    states = ("grp", s_send, s_recv, s_ss, s_rs, pl.ds(0, 48))
    states2 = ("grp", s_send, s_recv, s2_ss, s2_rs, pl.ds(48, 32))

    def send_states(part):
        for other in targets("grp"):

            @pl.when(other < TILES)
            def _(other=other):
                message(*part, other).start()

    send_states(states)
    f1_recv[b] = f1_send[b]
    h1_recv[g] = h1_send[g]

    def relay(src, dst, mid):
        mid[...] = src[...].reshape(512, 128).astype(F32)
        for k in range(N):
            for j in range(2):
                dst[k, 16 * j : 16 * j + 16, :] = mid[pl.ds(16 * j + k, N, stride=32), :].astype(BF16)

    f1_wait()
    relay(f1_recv, f2_send, mid)
    f2_start()
    send_states(states2)
    f2_recv[g] = f2_send[g]
    h1_wait()
    relay(h1_recv, h2_send, mid2)
    h2_start()
    h2_recv[b] = h2_send[b]

    loads[5].wait()
    loads[7].wait()
    p = pair_s[g * N + b]
    loads[2].wait()
    legb[0:512, :] = leg[0:512].reshape(512, 384).astype(BF16)
    last = jnp.where(
        lax.broadcasted_iota(jnp.int32, (16, 384), 0) == 0, jnp.broadcast_to(leg[512], (16, 384)), 0.0
    )
    legb[512:528, :] = last.astype(BF16)
    legt[:, 0:512] = leg[0:512].reshape(512, 384).T.astype(BF16)
    legt[:, 512:528] = last.T.astype(BF16)
    lane = lax.broadcasted_iota(jnp.int32, (1, 384), 1)
    chan = (lane % N) * C5 + jnp.minimum(2 * (lane // 128) + (lane % 128) // 64, C5 - 1)
    damping = jnp.zeros((1, 384), F32)
    for k in range(80):
        damping = jnp.where(chan == k, diff_s[k], damping)
    row = lax.broadcasted_iota(jnp.int32, (ROWS, 384), 0)
    first = row < M - p
    degree = jnp.where(first, p + row, row - 1).astype(F32)
    scaled = degree * (degree + 1.0) / F32(M * (M + 1))
    low = (lane % 64) < 32
    weight = jnp.where(low & (p == 0), F32(1.0 / NLON), F32(2.0 / NLON))
    fac[...] = jnp.where(first == low, jnp.exp(-damping * scaled) * weight, 0.0)
    loads[3].wait()
    loads[4].wait()
    wint[...] = (win[...].astype(F32) * 0.5).T.astype(BF16)

    tendencies = ("grp", t_send, t_recv, t_ss, t_rs, pl.ds(0, 32))
    tendencies2 = ("grp", t_send, t_recv, t2_ss, t2_rs, pl.ds(32, 48))

    def column_half(buffer):
        for i in range(8):
            xb[:, 128 * i : 128 * i + 128] = buffer[pl.ds(i, 80, stride=8), :].astype(BF16)
        half = lax.dot_general(wint[...], xb[...], nn, preferred_element_type=F32)
        hidden = (half + half * jnp.tanh(half)).astype(BF16)
        tend = lax.dot_general(woutt[...], hidden, nn, preferred_element_type=F32)
        for i in range(8):
            buffer[pl.ds(i, 80, stride=8), :] = tend[:, 128 * i : 128 * i + 128]

    @pl.when(g < TILES)
    def _():
        s_recv[g] = s_send[g]
        bulk(*states, N - 1).wait_recv()
        phys[...] = s_recv[:, 0:48, :].astype(F32)[:, 0:40].reshape(640, 128)
        column_half(phys)
        t_send[:, 0:32, :] = phys[...].reshape(N, 40, 128)[:, 0:32].astype(BF16)
        for other in reversed(targets("grp")):
            message(*tendencies, other).start()

    f1_sent()

    @pl.when(g < TILES)
    def _():
        bulk(*states, TILES - 1).wait_send()
        bulk(*states2, TILES - 1).wait_send()

    @pl.when(g >= TILES)
    def _():
        bulk(*states, TILES).wait_send()
        bulk(*states2, TILES).wait_send()

    h1_sent()
    f2_wait()
    mid[...] = f2_recv[...].reshape(512, 128).astype(F32)
    h2_wait()
    left = lax.broadcasted_iota(jnp.int32, (LAT, 128), 1) < 64
    for k in range(N):
        part = jnp.concatenate([mid[pl.ds(16 * j + k, N, stride=32), :] for j in range(2)] + [h2_recv[k].astype(F32)], 0)
        turned = jnp.concatenate([part, part], 0).T
        at = slice(LAT * k, LAT * k + LAT)
        zf[at, 0:128] = jnp.where(left, turned[0:24], turned[24:48])
        zf[at, 128:256] = jnp.where(left, turned[48:72], turned[72:96])
        zf[at, 256:384] = turned[96:120]
    proj = lax.dot_general(legb[...], zf[...].astype(BF16), nn, preferred_element_type=F32)
    spec = (proj * fac[...]).astype(BF16)
    zf[...] = lax.dot_general(legt[...], spec, nn, preferred_element_type=F32)
    lanes = lax.broadcasted_iota(jnp.int32, (64, 128), 1)
    odd_chan = ((lanes // LAT) % 2) == 1
    for k in range(N):
        at = slice(LAT * k, LAT * k + LAT)
        t0, t1, t2 = zf[at, 0:128], zf[at, 128:256], zf[at, 256:384]
        turned = jnp.concatenate([t0, t0, t1, t1, t2, jnp.zeros((8, 128), F32)], 0).T
        turned = jnp.where(odd_chan, turned[64:128], turned[0:64])
        b1_send[k] = turned[0:32].astype(BF16)
        mid2[32 * k : 32 * k + 32, :] = turned[32:64]
    for k in range(N):
        for j in range(2):
            c1_send[k, 16 * j : 16 * j + 16, :] = mid2[pl.ds(16 * j + k, N, stride=32), :].astype(BF16)

    b1_start, b1_wait, b1_sent = exchange("band", b1_send, b1_recv, b1_ss, b1_rs)
    b2_start, b2_wait, b2_sent = exchange("grp", b2_send, b2_recv, b2_ss, b2_rs)
    c1_start, c1_wait, c1_sent = exchange("grp", c1_send, c1_recv, c1_ss, c1_rs)
    c2_start, c2_wait, c2_sent = exchange("band", c2_send, c2_recv, c2_ss, c2_rs)
    c1_start()
    b1_start()
    b1_recv[b] = b1_send[b]
    c1_recv[g] = c1_send[g]

    @pl.when(g < TILES)
    def _():
        bulk(*states2, N - 1).wait_recv()
        phys2[...] = s_recv[:, 32:80, :].astype(F32)[:, 8:48].reshape(640, 128)
        column_half(phys2)
        rest = jnp.concatenate([phys[...].reshape(N, 40, 128)[:, 32:40], phys2[...].reshape(N, 40, 128)], axis=1)
        t_send[:, 32:80, :] = rest.astype(BF16)
        for other in reversed(targets("grp")):
            message(*tendencies2, other).start()
        t_recv[g] = t_send[g]

    f2_sent()
    h2_sent()
    b1_wait()
    relay(b1_recv, b2_send, mid)
    b2_start()
    b2_recv[g] = b2_send[g]
    c1_wait()
    relay(c1_recv, c2_send, mid2)
    c2_start()
    c2_recv[b] = c2_send[b]

    @pl.when(g < TILES)
    def _():
        bulk(*tendencies, TILES - 1).wait_recv()
        bulk(*tendencies2, TILES - 1).wait_recv()
        bulk(*tendencies, N - 1).wait_send()
        bulk(*tendencies2, N - 1).wait_send()

    @pl.when(g >= TILES)
    def _():
        bulk(*tendencies, TILES).wait_recv()
        bulk(*tendencies2, TILES).wait_recv()

    for a in range(3):
        for lp in range(5):
            block = t_recv[a * 5 + lp].astype(F32)
            out_ref[:, 8 * a : 8 * a + 8, 256 * lp : 256 * lp + 128] = block[0:40].reshape(C5, 8, 128)
            out_ref[:, 8 * a : 8 * a + 8, 256 * lp + 128 : 256 * lp + 256] = block[40:80].reshape(C5, 8, 128)

    b1_sent()
    c1_sent()
    b2_wait()
    c2_wait()
    natural = []
    for j in range(4):
        src, order = (b2_recv, oh) if j < 2 else (c2_recv, ohbg)
        at = 16 * (j % 2)
        slots = src[:, at : at + 16, :].reshape(256, 128).astype(F32).T.astype(BF16)
        natural.append(lax.dot_general(slots, order[...], nn, preferred_element_type=F32).astype(BF16))
    n0, n1, n2, n3 = natural
    even = jnp.concatenate([n0[:, :128], n1[:, :128], n2[:, 128:], n3[:, 128:]], 1)
    odd = jnp.concatenate([n0[:, 128:], n1[:, 128:], n2[:, :128], n3[:, :128]], 1)
    even = lax.dot_general(even, tab[:512, :], nn, preferred_element_type=F32)
    odd = lax.dot_general(odd, tab[512:, :], nn, preferred_element_type=F32)
    west = (even + odd)[:120].reshape(C5, LAT, HALF)
    east = (even - odd)[:120].reshape(C5, LAT, HALF)
    out_ref[:, :, :HALF] += west
    out_ref[:, :, HALF:] += east

    b2_sent()
    c2_sent()


def shards(state, pair_of_slot, legendre, diffusion, w_in, w_out):
    far = lambda x: pltpu.with_memory_space_constraint(x, pltpu.HBM)
    table = jnp.asarray(transform_table())
    hbm = pl.BlockSpec(memory_space=pltpu.HBM)
    vmem = pl.BlockSpec(memory_space=pltpu.VMEM)
    dma = pltpu.SemaphoreType.DMA
    message = pltpu.VMEM((N, 32, 128), BF16)
    block = pltpu.VMEM((N, 80, 128), BF16)
    return pl.pallas_call(
        kernel,
        out_shape=pltpu.VMEM(state.shape, F32),
        in_specs=[hbm] * 8,
        out_specs=vmem,
        scratch_shapes=[
            pltpu.VMEM(state.shape, F32),
            pltpu.VMEM((1024, HALF), BF16),
            pltpu.VMEM((513, 1, 384), F32),
            pltpu.VMEM((80, 1024), BF16),
            pltpu.VMEM((80, 1024), BF16),
            pltpu.SMEM((256,), jnp.int32),
            pltpu.VMEM((1, 256), jnp.int32),
            pltpu.SMEM((80,), F32),
            *[block] * 4,
            *[message] * 16,
            *[pltpu.VMEM((512, 128), F32)] * 2,
            *[pltpu.VMEM((640, 128), F32)] * 2,
            pltpu.VMEM((80, 1024), BF16),
            pltpu.VMEM((384, 384), F32),
            pltpu.VMEM((ROWS, 384), F32),
            pltpu.VMEM((ROWS, 384), BF16),
            pltpu.VMEM((384, ROWS), BF16),
            pltpu.VMEM((1024, 80), BF16),
            pltpu.VMEM((512, 128), F32),
            pltpu.VMEM((256, 256), BF16),
            pltpu.VMEM((256, 256), BF16),
            dma((8,)),
            *[dma] * 24,
        ],
        compiler_params=pltpu.CompilerParams(
            collective_id=0, has_side_effects=True, vmem_limit_bytes=40 * 1024 * 1024
        ),
        cost_estimate=pl.CostEstimate(flops=2_500_000_000, bytes_accessed=4_000_000, transcendentals=2_400_000),
    )(
        far(state), far(pair_of_slot), far(pair_of_slot.reshape(1, 256)), far(jnp.swapaxes(legendre, 0, 1)),
        far(diffusion), far(w_in), far(w_out.T), far(table)
    )


def solution(mesh):
    return jax.shard_map(
        shards,
        mesh=mesh,
        in_specs=(P("grp", "band", None), P(), P(("grp", "band"), None, None), P(), P(), P()),
        out_specs=P("grp", "band", None),
        check_vma=False,
    )
```

```python
import math

import jax
import jax.numpy as jnp
import numpy as np
from jax import lax
from jax.experimental import pallas as pl
from jax.experimental.pallas import tpu as pltpu
from jax.sharding import PartitionSpec as P

NLON = 1280
HALF = NLON // 2
M = 512
C5 = 5
LAT = 24
N = 16
ROWS = 528
TILES = 15
F32 = jnp.float32
BF16 = jnp.bfloat16


def transform_table():
    q = np.arange(128)
    lon = np.arange(HALF)
    blocks = []
    for parity in (0, 1):
        for j in range(4):
            p = 2 * q + (parity if j < 2 else 1 - parity)
            m = p if j < 2 else M - 1 - p
            phase = 2.0 * np.pi * ((m[:, None] * lon[None, :]) % NLON) / NLON
            blocks.append(np.cos(phase) if j % 2 == 0 else -np.sin(phase))
    return np.concatenate(blocks, 0).astype(jnp.bfloat16)


def kernel(
    state_h, pair_h, pairv_h, leg_h, diff_h, win_h, woutt_h, tab_h,
    out_ref,
    st, tab, leg, win, woutt, pair_s, pair_v, diff_s,
    s_send, s_recv, t_send, t_recv,
    f1_send, f1_recv, f2_send, f2_recv, h1_send, h1_recv, h2_send, h2_recv,
    b1_send, b1_recv, b2_send, b2_recv, c1_send, c1_recv, c2_send, c2_recv,
    mid, mid2, phys, phys2, xb, zf, fac, legb, legt, wint, ohf, oh, ohbg,
    load_sem, s_ss, s_rs, t_ss, t_rs, s2_ss, s2_rs, t2_ss, t2_rs,
    f1_ss, f1_rs, f2_ss, f2_rs, h1_ss, h1_rs, h2_ss, h2_rs,
    b1_ss, b1_rs, b2_ss, b2_rs, c1_ss, c1_rs, c2_ss, c2_rs,
):
    g = lax.axis_index("grp")
    b = lax.axis_index("band")

    def targets(axis):
        if axis == "grp":
            steps = sorted(((x, z) for x in range(2) for z in range(8)), key=lambda s: -(2 * s[0] + min(s[1], 8 - s[1])))
            return [lax.rem(g // 8 + x, 2) * 8 + lax.rem(g % 8 + z, 8) for x, z in steps[:-1]]
        steps = sorted(
            ((y, x, c) for y in range(4) for x in range(2) for c in range(2)),
            key=lambda s: -(2 * min(s[0], 4 - s[0]) + 2 * s[1] + s[2]),
        )
        return [
            lax.rem(b // 4 + y, 4) * 4 + lax.rem(b // 2 % 2 + x, 2) * 2 + lax.rem(b % 2 + c, 2) for y, x, c in steps[:-1]
        ]

    barrier = pltpu.get_barrier_semaphore()
    for axis in ("grp", "band"):
        for other in targets(axis):
            pl.semaphore_signal(barrier, inc=1, device_id={axis: other}, device_id_type=pl.DeviceIdType.MESH)

    loads = [
        pltpu.make_async_copy(src, dst, load_sem.at[i])
        for i, (src, dst) in enumerate(
            [(state_h, st), (tab_h, tab), (leg_h, leg), (win_h, win), (woutt_h, woutt),
             (pair_h, pair_s), (pairv_h, pair_v), (diff_h, diff_s)]
        )
    ]
    for i in (6, 0, 1):
        loads[i].start()

    def message(axis, src, dst, ss, rs, rows, other):
        return pltpu.make_async_remote_copy(
            src_ref=src.at[other, rows], dst_ref=dst.at[{"grp": g, "band": b}[axis], rows], send_sem=ss, recv_sem=rs,
            device_id={axis: other}, device_id_type=pl.DeviceIdType.MESH,
        )

    def bulk(axis, src, dst, ss, rs, rows, count):
        return pltpu.make_async_remote_copy(
            src_ref=src.at[pl.ds(0, count), rows], dst_ref=dst.at[pl.ds(0, count), rows], send_sem=ss, recv_sem=rs,
            device_id={axis: lax.rem({"grp": g, "band": b}[axis] + 1, N)}, device_id_type=pl.DeviceIdType.MESH,
        )

    def exchange(*refs):
        refs = (*refs, pl.ds(0, 32))

        def start():
            for other in targets(refs[0]):
                message(*refs, other).start()

        return start, bulk(*refs, N - 1).wait_recv, bulk(*refs, N - 1).wait_send

    value = 2 * (lax.broadcasted_iota(jnp.int32, (256, 256), 0) % 128) + lax.broadcasted_iota(jnp.int32, (256, 256), 0) // 128
    loads[6].wait()
    hot = (value == pair_v[...]).astype(F32)
    for h in range(2):
        ohf[256 * h : 256 * h + 256, :] = hot[128 * h : 128 * h + 128, :].T
        oh[:, 128 * h : 128 * h + 128] = ohf[256 * h : 256 * h + 256, :].astype(BF16)
        for k in range(N):
            turned = ohf[pl.ds(256 * h + k, N, stride=N), :].astype(BF16)
            ohbg[k * N : (k + 1) * N, 128 * h : 128 * h + 128] = turned

    loads[0].wait()
    rows = st[...].reshape(C5 * LAT, NLON)
    west, east = rows[:, :HALF], rows[:, HALF:]
    pad = jnp.zeros((8, HALF), F32)

    def terms(value):
        value = jnp.concatenate([value, pad], 0)
        high = value.astype(BF16)
        return jnp.concatenate([high, (value - high.astype(F32)).astype(BF16)], 0)

    even, odd = terms(west + east), terms(west - east)
    loads[1].wait()
    nt = (((1,), (1,)), ((), ()))
    nn = (((1,), (0,)), ((), ()))
    ce = lax.dot_general(tab[:512, :], even, nt, preferred_element_type=F32)
    co = lax.dot_general(tab[512:, :], odd, nt, preferred_element_type=F32)
    ce = (ce[:, :128] + ce[:, 128:]).astype(BF16)
    co = (co[:, :128] + co[:, 128:]).astype(BF16)
    for j in range(4):
        e, o = ce[128 * j : 128 * j + 128], co[128 * j : 128 * j + 128]
        natural = jnp.concatenate([e, o] if j < 2 else [o, e], 0)
        order, dst = (ohbg, f1_send) if j < 2 else (oh, h1_send)
        slots = lax.dot_general(order[...], natural, nn, preferred_element_type=F32).astype(BF16)
        dst[:, 16 * (j % 2) : 16 * (j % 2) + 16, :] = slots.reshape(N, 16, 128)

    f1_start, f1_wait, f1_sent = exchange("band", f1_send, f1_recv, f1_ss, f1_rs)
    f2_start, f2_wait, f2_sent = exchange("grp", f2_send, f2_recv, f2_ss, f2_rs)
    h1_start, h1_wait, h1_sent = exchange("grp", h1_send, h1_recv, h1_ss, h1_rs)
    h2_start, h2_wait, h2_sent = exchange("band", h2_send, h2_recv, h2_ss, h2_rs)
    pl.semaphore_wait(barrier, 2 * (N - 1))
    h1_start()
    f1_start()
    for i in (2, 3, 4, 5, 7):
        loads[i].start()

    for a in range(3):
        for lp in range(5):
            block = st[:, 8 * a : 8 * a + 8, 256 * lp : 256 * lp + 256]
            stacked = jnp.concatenate([block[:, :, :128], block[:, :, 128:]], axis=0)
            s_send[a * 5 + lp] = stacked.reshape(80, 128).astype(BF16)

    states = ("grp", s_send, s_recv, s_ss, s_rs, pl.ds(0, 48))
    states2 = ("grp", s_send, s_recv, s2_ss, s2_rs, pl.ds(48, 32))

    def send_states(part):
        for other in targets("grp"):

            @pl.when(other < TILES)
            def _(other=other):
                message(*part, other).start()

    send_states(states)
    f1_recv[b] = f1_send[b]
    h1_recv[g] = h1_send[g]

    def relay(src, dst, mid):
        mid[...] = src[...].reshape(512, 128).astype(F32)
        for k in range(N):
            for j in range(2):
                dst[k, 16 * j : 16 * j + 16, :] = mid[pl.ds(16 * j + k, N, stride=32), :].astype(BF16)

    f1_wait()
    relay(f1_recv, f2_send, mid)
    f2_start()
    send_states(states2)
    f2_recv[g] = f2_send[g]
    h1_wait()
    relay(h1_recv, h2_send, mid2)
    h2_start()
    h2_recv[b] = h2_send[b]

    loads[5].wait()
    loads[7].wait()
    p = pair_s[g * N + b]
    loads[2].wait()
    legb[0:512, :] = leg[0:512].reshape(512, 384).astype(BF16)
    last = jnp.where(
        lax.broadcasted_iota(jnp.int32, (16, 384), 0) == 0, jnp.broadcast_to(leg[512], (16, 384)), 0.0
    )
    legb[512:528, :] = last.astype(BF16)
    legt[:, 0:512] = leg[0:512].reshape(512, 384).T.astype(BF16)
    legt[:, 512:528] = last.T.astype(BF16)
    lane = lax.broadcasted_iota(jnp.int32, (1, 384), 1)
    chan = (lane % N) * C5 + jnp.minimum(2 * (lane // 128) + (lane % 128) // 64, C5 - 1)
    damping = jnp.zeros((1, 384), F32)
    for k in range(80):
        damping = jnp.where(chan == k, diff_s[k], damping)
    row = lax.broadcasted_iota(jnp.int32, (ROWS, 384), 0)
    first = row < M - p
    degree = jnp.where(first, p + row, row - 1).astype(F32)
    scaled = degree * (degree + 1.0) / F32(M * (M + 1))
    low = (lane % 64) < 32
    weight = jnp.where(low & (p == 0), F32(1.0 / NLON), F32(2.0 / NLON))
    fac[...] = jnp.where(first == low, jnp.exp(-damping * scaled) * weight, 0.0)
    loads[3].wait()
    loads[4].wait()
    wint[...] = (win[...].astype(F32) * 0.5).T.astype(BF16)

    tendencies = ("grp", t_send, t_recv, t_ss, t_rs, pl.ds(0, 32))
    tendencies2 = ("grp", t_send, t_recv, t2_ss, t2_rs, pl.ds(32, 48))

    def column_half(buffer):
        for i in range(8):
            xb[:, 128 * i : 128 * i + 128] = buffer[pl.ds(i, 80, stride=8), :].astype(BF16)
        half = lax.dot_general(wint[...], xb[...], nn, preferred_element_type=F32)
        hidden = (half + half * jnp.tanh(half)).astype(BF16)
        tend = lax.dot_general(woutt[...], hidden, nn, preferred_element_type=F32)
        for i in range(8):
            buffer[pl.ds(i, 80, stride=8), :] = tend[:, 128 * i : 128 * i + 128]

    @pl.when(g < TILES)
    def _():
        s_recv[g] = s_send[g]
        bulk(*states, N - 1).wait_recv()
        phys[...] = s_recv[:, 0:48, :].astype(F32)[:, 0:40].reshape(640, 128)
        column_half(phys)
        t_send[:, 0:32, :] = phys[...].reshape(N, 40, 128)[:, 0:32].astype(BF16)
        for other in reversed(targets("grp")):
            message(*tendencies, other).start()

    f1_sent()

    @pl.when(g < TILES)
    def _():
        bulk(*states, TILES - 1).wait_send()
        bulk(*states2, TILES - 1).wait_send()

    @pl.when(g >= TILES)
    def _():
        bulk(*states, TILES).wait_send()
        bulk(*states2, TILES).wait_send()

    h1_sent()
    f2_wait()
    mid[...] = f2_recv[...].reshape(512, 128).astype(F32)
    h2_wait()
    left = lax.broadcasted_iota(jnp.int32, (LAT, 128), 1) < 64
    for k in range(N):
        part = jnp.concatenate([mid[pl.ds(16 * j + k, N, stride=32), :] for j in range(2)] + [h2_recv[k].astype(F32)], 0)
        turned = jnp.concatenate([part, part], 0).T
        at = slice(LAT * k, LAT * k + LAT)
        zf[at, 0:128] = jnp.where(left, turned[0:24], turned[24:48])
        zf[at, 128:256] = jnp.where(left, turned[48:72], turned[72:96])
        zf[at, 256:384] = turned[96:120]
    proj = lax.dot_general(legb[...], zf[...].astype(BF16), nn, preferred_element_type=F32)
    spec = (proj * fac[...]).astype(BF16)
    zf[...] = lax.dot_general(legt[...], spec, nn, preferred_element_type=F32)
    lanes = lax.broadcasted_iota(jnp.int32, (64, 128), 1)
    odd_chan = ((lanes // LAT) % 2) == 1
    for k in range(N):
        at = slice(LAT * k, LAT * k + LAT)
        t0, t1, t2 = zf[at, 0:128], zf[at, 128:256], zf[at, 256:384]
        turned = jnp.concatenate([t0, t0, t1, t1, t2, jnp.zeros((8, 128), F32)], 0).T
        turned = jnp.where(odd_chan, turned[64:128], turned[0:64])
        b1_send[k] = turned[0:32].astype(BF16)
        mid2[32 * k : 32 * k + 32, :] = turned[32:64]
    for k in range(N):
        for j in range(2):
            c1_send[k, 16 * j : 16 * j + 16, :] = mid2[pl.ds(16 * j + k, N, stride=32), :].astype(BF16)

    b1_start, b1_wait, b1_sent = exchange("band", b1_send, b1_recv, b1_ss, b1_rs)
    b2_start, b2_wait, b2_sent = exchange("grp", b2_send, b2_recv, b2_ss, b2_rs)
    c1_start, c1_wait, c1_sent = exchange("grp", c1_send, c1_recv, c1_ss, c1_rs)
    c2_start, c2_wait, c2_sent = exchange("band", c2_send, c2_recv, c2_ss, c2_rs)
    c1_start()
    b1_start()
    b1_recv[b] = b1_send[b]
    c1_recv[g] = c1_send[g]

    @pl.when(g < TILES)
    def _():
        bulk(*states2, N - 1).wait_recv()
        phys2[...] = s_recv[:, 32:80, :].astype(F32)[:, 8:48].reshape(640, 128)
        column_half(phys2)
        rest = jnp.concatenate([phys[...].reshape(N, 40, 128)[:, 32:40], phys2[...].reshape(N, 40, 128)], axis=1)
        t_send[:, 32:80, :] = rest.astype(BF16)
        for other in reversed(targets("grp")):
            message(*tendencies2, other).start()
        t_recv[g] = t_send[g]

    f2_sent()
    h2_sent()
    b1_wait()
    relay(b1_recv, b2_send, mid)
    b2_start()
    b2_recv[g] = b2_send[g]
    c1_wait()
    relay(c1_recv, c2_send, mid2)
    c2_start()
    c2_recv[b] = c2_send[b]

    @pl.when(g < TILES)
    def _():
        bulk(*tendencies, TILES - 1).wait_recv()
        bulk(*tendencies2, TILES - 1).wait_recv()
        bulk(*tendencies, N - 1).wait_send()
        bulk(*tendencies2, N - 1).wait_send()

    @pl.when(g >= TILES)
    def _():
        bulk(*tendencies, TILES).wait_recv()
        bulk(*tendencies2, TILES).wait_recv()

    for a in range(3):
        for lp in range(5):
            block = t_recv[a * 5 + lp].astype(F32)
            out_ref[:, 8 * a : 8 * a + 8, 256 * lp : 256 * lp + 128] = block[0:40].reshape(C5, 8, 128)
            out_ref[:, 8 * a : 8 * a + 8, 256 * lp + 128 : 256 * lp + 256] = block[40:80].reshape(C5, 8, 128)

    b1_sent()
    c1_sent()
    b2_wait()
    c2_wait()
    natural = []
    for j in range(4):
        src, order = (b2_recv, oh) if j < 2 else (c2_recv, ohbg)
        at = 16 * (j % 2)
        slots = src[:, at : at + 16, :].reshape(256, 128).astype(F32).T.astype(BF16)
        natural.append(lax.dot_general(slots, order[...], nn, preferred_element_type=F32).astype(BF16))
    n0, n1, n2, n3 = natural
    even = jnp.concatenate([n0[:, :128], n1[:, :128], n2[:, 128:], n3[:, 128:]], 1)
    odd = jnp.concatenate([n0[:, 128:], n1[:, 128:], n2[:, :128], n3[:, :128]], 1)
    even = lax.dot_general(even, tab[:512, :], nn, preferred_element_type=F32)
    odd = lax.dot_general(odd, tab[512:, :], nn, preferred_element_type=F32)
    west = (even + odd)[:120].reshape(C5, LAT, HALF)
    east = (even - odd)[:120].reshape(C5, LAT, HALF)
    out_ref[:, :, :HALF] += west
    out_ref[:, :, HALF:] += east

    b2_sent()
    c2_sent()


def shards(state, pair_of_slot, legendre, diffusion, w_in, w_out):
    far = lambda x: pltpu.with_memory_space_constraint(x, pltpu.HBM)
    table = jnp.asarray(transform_table())
    hbm = pl.BlockSpec(memory_space=pltpu.HBM)
    vmem = pl.BlockSpec(memory_space=pltpu.VMEM)
    dma = pltpu.SemaphoreType.DMA
    message = pltpu.VMEM((N, 32, 128), BF16)
    block = pltpu.VMEM((N, 80, 128), BF16)
    return pl.pallas_call(
        kernel,
        out_shape=pltpu.VMEM(state.shape, F32),
        in_specs=[hbm] * 8,
        out_specs=vmem,
        scratch_shapes=[
            pltpu.VMEM(state.shape, F32),
            pltpu.VMEM((1024, HALF), BF16),
            pltpu.VMEM((513, 1, 384), F32),
            pltpu.VMEM((80, 1024), BF16),
            pltpu.VMEM((80, 1024), BF16),
            pltpu.SMEM((256,), jnp.int32),
            pltpu.VMEM((1, 256), jnp.int32),
            pltpu.SMEM((80,), F32),
            *[block] * 4,
            *[message] * 16,
            *[pltpu.VMEM((512, 128), F32)] * 2,
            *[pltpu.VMEM((640, 128), F32)] * 2,
            pltpu.VMEM((80, 1024), BF16),
            pltpu.VMEM((384, 384), F32),
            pltpu.VMEM((ROWS, 384), F32),
            pltpu.VMEM((ROWS, 384), BF16),
            pltpu.VMEM((384, ROWS), BF16),
            pltpu.VMEM((1024, 80), BF16),
            pltpu.VMEM((512, 128), F32),
            pltpu.VMEM((256, 256), BF16),
            pltpu.VMEM((256, 256), BF16),
            dma((8,)),
            *[dma] * 24,
        ],
        compiler_params=pltpu.CompilerParams(
            collective_id=0, has_side_effects=True, vmem_limit_bytes=40 * 1024 * 1024
        ),
        cost_estimate=pl.CostEstimate(flops=2_500_000_000, bytes_accessed=4_000_000, transcendentals=2_400_000),
    )(
        far(state), far(pair_of_slot), far(pair_of_slot.reshape(1, 256)), far(jnp.swapaxes(legendre, 0, 1)),
        far(diffusion), far(w_in), far(w_out.T), far(table)
    )


def solution(mesh):
    return jax.shard_map(
        shards,
        mesh=mesh,
        in_specs=(P("grp", "band", None), P(), P(("grp", "band"), None, None), P(), P(), P()),
        out_specs=P("grp", "band", None),
        check_vma=False,
    )
```

```python
import math

import jax
import jax.numpy as jnp
import numpy as np
from jax import lax
from jax.experimental import pallas as pl
from jax.experimental.pallas import tpu as pltpu
from jax.sharding import PartitionSpec as P

NLON = 1280
HALF = NLON // 2
M = 512
C5 = 5
LAT = 24
N = 16
ROWS = 528
TILES = 15
F32 = jnp.float32
BF16 = jnp.bfloat16


def transform_table():
    q = np.arange(128)
    lon = np.arange(HALF)
    blocks = []
    for parity in (0, 1):
        for j in range(4):
            p = 2 * q + (parity if j < 2 else 1 - parity)
            m = p if j < 2 else M - 1 - p
            phase = 2.0 * np.pi * ((m[:, None] * lon[None, :]) % NLON) / NLON
            blocks.append(np.cos(phase) if j % 2 == 0 else -np.sin(phase))
    return np.concatenate(blocks, 0).astype(jnp.bfloat16)


def kernel(
    state_h, pair_h, pairv_h, leg_h, diff_h, win_h, woutt_h, tab_h,
    out_ref,
    st, tab, leg, win, woutt, pair_s, pair_v, diff_s,
    s_send, s_recv, t_send, t_recv,
    f1_send, f1_recv, f2_send, f2_recv, h1_send, h1_recv, h2_send, h2_recv,
    b1_send, b1_recv, b2_send, b2_recv, c1_send, c1_recv, c2_send, c2_recv,
    mid, mid2, phys, phys2, xb, zf, fac, legb, legt, wint, ohf, oh, ohbg,
    load_sem, s_ss, s_rs, t_ss, t_rs, s2_ss, s2_rs, t2_ss, t2_rs,
    f1_ss, f1_rs, f2_ss, f2_rs, h1_ss, h1_rs, h2_ss, h2_rs,
    b1_ss, b1_rs, b2_ss, b2_rs, c1_ss, c1_rs, c2_ss, c2_rs,
):
    g = lax.axis_index("grp")
    b = lax.axis_index("band")

    def targets(axis):
        if axis == "grp":
            steps = sorted(((x, z) for x in range(2) for z in range(8)), key=lambda s: -(2 * s[0] + min(s[1], 8 - s[1])))
            return [lax.rem(g // 8 + x, 2) * 8 + lax.rem(g % 8 + z, 8) for x, z in steps[:-1]]
        steps = sorted(
            ((y, x, c) for y in range(4) for x in range(2) for c in range(2)),
            key=lambda s: -(2 * min(s[0], 4 - s[0]) + 2 * s[1] + s[2]),
        )
        return [
            lax.rem(b // 4 + y, 4) * 4 + lax.rem(b // 2 % 2 + x, 2) * 2 + lax.rem(b % 2 + c, 2) for y, x, c in steps[:-1]
        ]

    barrier = pltpu.get_barrier_semaphore()
    for axis in ("grp", "band"):
        for other in targets(axis):
            pl.semaphore_signal(barrier, inc=1, device_id={axis: other}, device_id_type=pl.DeviceIdType.MESH)

    loads = [
        pltpu.make_async_copy(src, dst, load_sem.at[i])
        for i, (src, dst) in enumerate(
            [(state_h, st), (tab_h, tab), (leg_h, leg), (win_h, win), (woutt_h, woutt),
             (pair_h, pair_s), (pairv_h, pair_v), (diff_h, diff_s)]
        )
    ]
    for i in (6, 0, 1):
        loads[i].start()

    def message(axis, src, dst, ss, rs, rows, other):
        return pltpu.make_async_remote_copy(
            src_ref=src.at[other, rows], dst_ref=dst.at[{"grp": g, "band": b}[axis], rows], send_sem=ss, recv_sem=rs,
            device_id={axis: other}, device_id_type=pl.DeviceIdType.MESH,
        )

    def bulk(axis, src, dst, ss, rs, rows, count):
        return pltpu.make_async_remote_copy(
            src_ref=src.at[pl.ds(0, count), rows], dst_ref=dst.at[pl.ds(0, count), rows], send_sem=ss, recv_sem=rs,
            device_id={axis: lax.rem({"grp": g, "band": b}[axis] + 1, N)}, device_id_type=pl.DeviceIdType.MESH,
        )

    def exchange(*refs):
        refs = (*refs, pl.ds(0, 32))

        def start():
            for other in targets(refs[0]):
                message(*refs, other).start()

        return start, bulk(*refs, N - 1).wait_recv, bulk(*refs, N - 1).wait_send

    value = 2 * (lax.broadcasted_iota(jnp.int32, (256, 256), 0) % 128) + lax.broadcasted_iota(jnp.int32, (256, 256), 0) // 128
    loads[6].wait()
    hot = (value == pair_v[...]).astype(F32)
    for h in range(2):
        ohf[256 * h : 256 * h + 256, :] = hot[128 * h : 128 * h + 128, :].T
        oh[:, 128 * h : 128 * h + 128] = ohf[256 * h : 256 * h + 256, :].astype(BF16)
        for k in range(N):
            turned = ohf[pl.ds(256 * h + k, N, stride=N), :].astype(BF16)
            ohbg[k * N : (k + 1) * N, 128 * h : 128 * h + 128] = turned

    loads[0].wait()
    rows = st[...].reshape(C5 * LAT, NLON)
    west, east = rows[:, :HALF], rows[:, HALF:]
    pad = jnp.zeros((8, HALF), F32)

    def terms(value):
        value = jnp.concatenate([value, pad], 0)
        high = value.astype(BF16)
        return jnp.concatenate([high, (value - high.astype(F32)).astype(BF16)], 0)

    even, odd = terms(west + east), terms(west - east)
    loads[1].wait()
    nt = (((1,), (1,)), ((), ()))
    nn = (((1,), (0,)), ((), ()))
    ce = lax.dot_general(tab[:512, :], even, nt, preferred_element_type=F32)
    co = lax.dot_general(tab[512:, :], odd, nt, preferred_element_type=F32)
    ce = (ce[:, :128] + ce[:, 128:]).astype(BF16)
    co = (co[:, :128] + co[:, 128:]).astype(BF16)
    for j in range(4):
        e, o = ce[128 * j : 128 * j + 128], co[128 * j : 128 * j + 128]
        natural = jnp.concatenate([e, o] if j < 2 else [o, e], 0)
        order, dst = (ohbg, f1_send) if j < 2 else (oh, h1_send)
        slots = lax.dot_general(order[...], natural, nn, preferred_element_type=F32).astype(BF16)
        dst[:, 16 * (j % 2) : 16 * (j % 2) + 16, :] = slots.reshape(N, 16, 128)

    f1_start, f1_wait, f1_sent = exchange("band", f1_send, f1_recv, f1_ss, f1_rs)
    f2_start, f2_wait, f2_sent = exchange("grp", f2_send, f2_recv, f2_ss, f2_rs)
    h1_start, h1_wait, h1_sent = exchange("grp", h1_send, h1_recv, h1_ss, h1_rs)
    h2_start, h2_wait, h2_sent = exchange("band", h2_send, h2_recv, h2_ss, h2_rs)
    for a in range(3):
        for lp in range(5):
            block = st[:, 8 * a : 8 * a + 8, 256 * lp : 256 * lp + 256]
            stacked = jnp.concatenate([block[:, :, :128], block[:, :, 128:]], axis=0)
            s_send[a * 5 + lp] = stacked.reshape(80, 128).astype(BF16)

    pl.semaphore_wait(barrier, 2 * (N - 1))
    h1_start()
    f1_start()
    for i in (2, 3, 4, 5, 7):
        loads[i].start()

    states = ("grp", s_send, s_recv, s_ss, s_rs, pl.ds(0, 48))
    states2 = ("grp", s_send, s_recv, s2_ss, s2_rs, pl.ds(48, 32))

    def send_states(part):
        for other in targets("grp"):

            @pl.when(other < TILES)
            def _(other=other):
                message(*part, other).start()

    send_states(states)
    f1_recv[b] = f1_send[b]
    h1_recv[g] = h1_send[g]

    def relay(src, dst, mid):
        mid[...] = src[...].reshape(512, 128).astype(F32)
        for k in range(N):
            for j in range(2):
                dst[k, 16 * j : 16 * j + 16, :] = mid[pl.ds(16 * j + k, N, stride=32), :].astype(BF16)

    f1_wait()
    relay(f1_recv, f2_send, mid)
    f2_start()
    send_states(states2)
    f2_recv[g] = f2_send[g]
    h1_wait()
    relay(h1_recv, h2_send, mid2)
    h2_start()
    h2_recv[b] = h2_send[b]

    loads[5].wait()
    loads[7].wait()
    p = pair_s[g * N + b]
    loads[2].wait()
    legb[0:512, :] = leg[0:512].reshape(512, 384).astype(BF16)
    last = jnp.where(
        lax.broadcasted_iota(jnp.int32, (16, 384), 0) == 0, jnp.broadcast_to(leg[512], (16, 384)), 0.0
    )
    legb[512:528, :] = last.astype(BF16)
    legt[:, 0:512] = leg[0:512].reshape(512, 384).T.astype(BF16)
    legt[:, 512:528] = last.T.astype(BF16)
    lane = lax.broadcasted_iota(jnp.int32, (1, 384), 1)
    chan = (lane % N) * C5 + jnp.minimum(2 * (lane // 128) + (lane % 128) // 64, C5 - 1)
    damping = jnp.zeros((1, 384), F32)
    for k in range(80):
        damping = jnp.where(chan == k, diff_s[k], damping)
    row = lax.broadcasted_iota(jnp.int32, (ROWS, 384), 0)
    first = row < M - p
    degree = jnp.where(first, p + row, row - 1).astype(F32)
    scaled = degree * (degree + 1.0) / F32(M * (M + 1))
    low = (lane % 64) < 32
    weight = jnp.where(low & (p == 0), F32(1.0 / NLON), F32(2.0 / NLON))
    fac[...] = jnp.where(first == low, jnp.exp(-damping * scaled) * weight, 0.0)
    loads[3].wait()
    loads[4].wait()
    wint[...] = (win[...].astype(F32) * 0.5).T.astype(BF16)

    tendencies = ("grp", t_send, t_recv, t_ss, t_rs, pl.ds(0, 32))
    tendencies2 = ("grp", t_send, t_recv, t2_ss, t2_rs, pl.ds(32, 48))

    def column_half(buffer):
        for i in range(8):
            xb[:, 128 * i : 128 * i + 128] = buffer[pl.ds(i, 80, stride=8), :].astype(BF16)
        half = lax.dot_general(wint[...], xb[...], nn, preferred_element_type=F32)
        hidden = (half + half * jnp.tanh(half)).astype(BF16)
        tend = lax.dot_general(woutt[...], hidden, nn, preferred_element_type=F32)
        for i in range(8):
            buffer[pl.ds(i, 80, stride=8), :] = tend[:, 128 * i : 128 * i + 128]

    @pl.when(g < TILES)
    def _():
        s_recv[g] = s_send[g]
        bulk(*states, N - 1).wait_recv()
        phys[...] = s_recv[:, 0:48, :].astype(F32)[:, 0:40].reshape(640, 128)
        column_half(phys)
        t_send[:, 0:32, :] = phys[...].reshape(N, 40, 128)[:, 0:32].astype(BF16)
        for other in reversed(targets("grp")):
            message(*tendencies, other).start()

    f1_sent()

    @pl.when(g < TILES)
    def _():
        bulk(*states, TILES - 1).wait_send()
        bulk(*states2, TILES - 1).wait_send()

    @pl.when(g >= TILES)
    def _():
        bulk(*states, TILES).wait_send()
        bulk(*states2, TILES).wait_send()

    h1_sent()
    f2_wait()
    mid[...] = f2_recv[...].reshape(512, 128).astype(F32)
    h2_wait()
    left = lax.broadcasted_iota(jnp.int32, (LAT, 128), 1) < 64
    for k in range(N):
        part = jnp.concatenate([mid[pl.ds(16 * j + k, N, stride=32), :] for j in range(2)] + [h2_recv[k].astype(F32)], 0)
        turned = jnp.concatenate([part, part], 0).T
        at = slice(LAT * k, LAT * k + LAT)
        zf[at, 0:128] = jnp.where(left, turned[0:24], turned[24:48])
        zf[at, 128:256] = jnp.where(left, turned[48:72], turned[72:96])
        zf[at, 256:384] = turned[96:120]
    proj = lax.dot_general(legb[...], zf[...].astype(BF16), nn, preferred_element_type=F32)
    spec = (proj * fac[...]).astype(BF16)
    zf[...] = lax.dot_general(legt[...], spec, nn, preferred_element_type=F32)
    lanes = lax.broadcasted_iota(jnp.int32, (64, 128), 1)
    odd_chan = ((lanes // LAT) % 2) == 1
    for k in range(N):
        at = slice(LAT * k, LAT * k + LAT)
        t0, t1, t2 = zf[at, 0:128], zf[at, 128:256], zf[at, 256:384]
        turned = jnp.concatenate([t0, t0, t1, t1, t2, jnp.zeros((8, 128), F32)], 0).T
        turned = jnp.where(odd_chan, turned[64:128], turned[0:64])
        b1_send[k] = turned[0:32].astype(BF16)
        mid2[32 * k : 32 * k + 32, :] = turned[32:64]
    for k in range(N):
        for j in range(2):
            c1_send[k, 16 * j : 16 * j + 16, :] = mid2[pl.ds(16 * j + k, N, stride=32), :].astype(BF16)

    b1_start, b1_wait, b1_sent = exchange("band", b1_send, b1_recv, b1_ss, b1_rs)
    b2_start, b2_wait, b2_sent = exchange("grp", b2_send, b2_recv, b2_ss, b2_rs)
    c1_start, c1_wait, c1_sent = exchange("grp", c1_send, c1_recv, c1_ss, c1_rs)
    c2_start, c2_wait, c2_sent = exchange("band", c2_send, c2_recv, c2_ss, c2_rs)
    c1_start()
    b1_start()
    b1_recv[b] = b1_send[b]
    c1_recv[g] = c1_send[g]

    @pl.when(g < TILES)
    def _():
        bulk(*states2, N - 1).wait_recv()
        phys2[...] = s_recv[:, 32:80, :].astype(F32)[:, 8:48].reshape(640, 128)
        column_half(phys2)
        rest = jnp.concatenate([phys[...].reshape(N, 40, 128)[:, 32:40], phys2[...].reshape(N, 40, 128)], axis=1)
        t_send[:, 32:80, :] = rest.astype(BF16)
        for other in reversed(targets("grp")):
            message(*tendencies2, other).start()
        t_recv[g] = t_send[g]

    f2_sent()
    h2_sent()
    b1_wait()
    relay(b1_recv, b2_send, mid)
    b2_start()
    b2_recv[g] = b2_send[g]
    c1_wait()
    relay(c1_recv, c2_send, mid2)
    c2_start()
    c2_recv[b] = c2_send[b]

    @pl.when(g < TILES)
    def _():
        bulk(*tendencies, TILES - 1).wait_recv()
        bulk(*tendencies2, TILES - 1).wait_recv()
        bulk(*tendencies, N - 1).wait_send()
        bulk(*tendencies2, N - 1).wait_send()

    @pl.when(g >= TILES)
    def _():
        bulk(*tendencies, TILES).wait_recv()
        bulk(*tendencies2, TILES).wait_recv()

    for a in range(3):
        for lp in range(5):
            block = t_recv[a * 5 + lp].astype(F32)
            out_ref[:, 8 * a : 8 * a + 8, 256 * lp : 256 * lp + 128] = block[0:40].reshape(C5, 8, 128)
            out_ref[:, 8 * a : 8 * a + 8, 256 * lp + 128 : 256 * lp + 256] = block[40:80].reshape(C5, 8, 128)

    b1_sent()
    c1_sent()
    b2_wait()
    c2_wait()
    natural = []
    for j in range(4):
        src, order = (b2_recv, oh) if j < 2 else (c2_recv, ohbg)
        at = 16 * (j % 2)
        slots = src[:, at : at + 16, :].reshape(256, 128).astype(F32).T.astype(BF16)
        natural.append(lax.dot_general(slots, order[...], nn, preferred_element_type=F32).astype(BF16))
    n0, n1, n2, n3 = natural
    even = jnp.concatenate([n0[:, :128], n1[:, :128], n2[:, 128:], n3[:, 128:]], 1)
    odd = jnp.concatenate([n0[:, 128:], n1[:, 128:], n2[:, :128], n3[:, :128]], 1)
    even = lax.dot_general(even, tab[:512, :], nn, preferred_element_type=F32)
    odd = lax.dot_general(odd, tab[512:, :], nn, preferred_element_type=F32)
    west = (even + odd)[:120].reshape(C5, LAT, HALF)
    east = (even - odd)[:120].reshape(C5, LAT, HALF)
    out_ref[:, :, :HALF] += west
    out_ref[:, :, HALF:] += east

    b2_sent()
    c2_sent()


def shards(state, pair_of_slot, legendre, diffusion, w_in, w_out):
    far = lambda x: pltpu.with_memory_space_constraint(x, pltpu.HBM)
    table = jnp.asarray(transform_table())
    hbm = pl.BlockSpec(memory_space=pltpu.HBM)
    vmem = pl.BlockSpec(memory_space=pltpu.VMEM)
    dma = pltpu.SemaphoreType.DMA
    message = pltpu.VMEM((N, 32, 128), BF16)
    block = pltpu.VMEM((N, 80, 128), BF16)
    return pl.pallas_call(
        kernel,
        out_shape=pltpu.VMEM(state.shape, F32),
        in_specs=[hbm] * 8,
        out_specs=vmem,
        scratch_shapes=[
            pltpu.VMEM(state.shape, F32),
            pltpu.VMEM((1024, HALF), BF16),
            pltpu.VMEM((513, 1, 384), F32),
            pltpu.VMEM((80, 1024), BF16),
            pltpu.VMEM((80, 1024), BF16),
            pltpu.SMEM((256,), jnp.int32),
            pltpu.VMEM((1, 256), jnp.int32),
            pltpu.SMEM((80,), F32),
            *[block] * 4,
            *[message] * 16,
            *[pltpu.VMEM((512, 128), F32)] * 2,
            *[pltpu.VMEM((640, 128), F32)] * 2,
            pltpu.VMEM((80, 1024), BF16),
            pltpu.VMEM((384, 384), F32),
            pltpu.VMEM((ROWS, 384), F32),
            pltpu.VMEM((ROWS, 384), BF16),
            pltpu.VMEM((384, ROWS), BF16),
            pltpu.VMEM((1024, 80), BF16),
            pltpu.VMEM((512, 128), F32),
            pltpu.VMEM((256, 256), BF16),
            pltpu.VMEM((256, 256), BF16),
            dma((8,)),
            *[dma] * 24,
        ],
        compiler_params=pltpu.CompilerParams(
            collective_id=0, has_side_effects=True, vmem_limit_bytes=40 * 1024 * 1024
        ),
        cost_estimate=pl.CostEstimate(flops=2_500_000_000, bytes_accessed=4_000_000, transcendentals=2_400_000),
    )(
        far(state), far(pair_of_slot), far(pair_of_slot.reshape(1, 256)), far(jnp.swapaxes(legendre, 0, 1)),
        far(diffusion), far(w_in), far(w_out.T), far(table)
    )


def solution(mesh):
    return jax.shard_map(
        shards,
        mesh=mesh,
        in_specs=(P("grp", "band", None), P(), P(("grp", "band"), None, None), P(), P(), P()),
        out_specs=P("grp", "band", None),
        check_vma=False,
    )
```
